256 devices in a mesh: rep: 16 (over y, x_hi, core), fsdp: 16 (over x_lo, z).
Axes of the slice: x: 4 (x_hi: 2, x_lo: 2; x = x_hi * 2 + x_lo), y: 4, z: 8, core: 2. Of those that a mesh axis runs over, the one named last changes fastest.
Arguments:
- inputs: bfloat16 [32768, 6656], P(('rep', 'fsdp')), may hold values from -40 to 40, as said below
- cotangent: bfloat16 [32768, 3328], P(('rep', 'fsdp')), may hold values from -6 to 6
- weight: bfloat16 [16, 6656, 3328], P('rep', 'fsdp'), may hold values from -6 to 6
- gain: bfloat16 [16, 6656], P('rep', 'fsdp'), may hold values from 0.25 to 1.75
- step: int32 [1], replicated, may hold values from 0 to 1048575
Outputs:
- input_gradient: bfloat16 [32768, 6656], P(('rep', 'fsdp'))
- weight_out: bfloat16 [16, 6656, 3328], P('rep', 'fsdp')
- gain_out: bfloat16 [16, 6656], P('rep', 'fsdp')
The draws below stay inside these ranges and needn't reach their ends.
Inputs may be any that keep to these rules, and one draw needn't show every extreme that they name: `inputs`: entries of order one times a per-token and a per-feature scale that differ over a factor of ten.
All inputs are finite; a program needn't handle non-finite values.
Results may differ from the reference program's by a relative error of at most 0.0053.
Values may be sent and summed in bfloat16 or wider, within the bound.
A program may use at most 128 MiB of HBM per device.

```python
import math
import jax
import jax.numpy as jnp
from jax import lax

D = 6656
HQ = 3328
TOKENS = 32768
LOG_REP = 4
N_REP = 16


def draw_inputs(key, part):
    key = jax.random.fold_in(key, 11)
    key_rows, key_cols, key_base = jax.random.split(key, 3)
    row_scale = jnp.exp(jax.random.uniform(key_rows, (TOKENS, 1), jnp.float32) * math.log(10.0))
    col_scale = jnp.exp(jax.random.uniform(key_cols, (1, D), jnp.float32) * math.log(10.0))
    base = jnp.clip(jax.random.normal(key_base, (TOKENS, D), jnp.float32), -3.5, 3.5)
    return (base * row_scale * col_scale / 20.0).astype(jnp.bfloat16)


def steps_of(own_key, dims, pieces, least, top_value):
    factor_of = 1.0
    for dim, shards_of in pieces:
        draws = jax.random.uniform(jax.random.fold_in(jax.random.fold_in(own_key, 6), dim), (shards_of,), jnp.float32, least / len(pieces), top_value / len(pieces))
        factor_of = factor_of * jnp.repeat(jnp.exp(draws), dims[dim] // shards_of).reshape((-1,) + (1,) * (len(dims) - 1 - dim))
    return factor_of


def centred(rng, shape, scale, reach, cuts=(), dtype=jnp.bfloat16):
    array = jax.random.normal(rng, shape, jnp.float32) * scale
    if len(cuts) > 0:
        array = steps_of(rng, shape, cuts, -0.22, 0.18) * array
    return jnp.clip(array, min=-reach, max=reach).astype(dtype)


def setup_inputs(seed: int = 0) -> dict:
    arg_keys = jax.random.split(jax.random.key(seed), 6)
    return {
        "inputs": draw_inputs(jax.random.fold_in(arg_keys[5], 71), 0),
        "cotangent": centred(arg_keys[1], (TOKENS, HQ), 1.0, 6.0, ((0, 256),)),
        "weight": centred(arg_keys[2], (N_REP, D, HQ), 1.0, 6.0, ((0, 16), (1, 16))),
        "gain": jnp.clip(1.0 + 0.15 * jax.random.normal(arg_keys[3], (N_REP, D), jnp.float32), 0.25, 1.75).astype(jnp.bfloat16),
        "step": jax.random.randint(arg_keys[4], (1,), 0, 1048576).astype(jnp.int32),
    }


epsilon = 1e-05
learn_rate = 0.5
gain_rate = 0.01

def one_replica(packed):
    inputs, cotangent, weight, gain = packed
    row_total = inputs.astype(jnp.float32)
    inverse_deviation = lax.rsqrt(lax.optimization_barrier(jnp.mean(row_total * row_total, axis=-1, keepdims=True)) + epsilon)
    normalized_input = lax.optimization_barrier((row_total * inverse_deviation).astype(jnp.bfloat16))
    normalized_input_wide = normalized_input.astype(jnp.float32)
    gain_wide = gain.astype(jnp.float32)
    scaled_rows = (normalized_input_wide * gain_wide).astype(jnp.bfloat16)
    factor = D ** (-0.5)
    wgrad = factor * jnp.dot(scaled_rows.T, cotangent, preferred_element_type=jnp.float32)
    feature_gradient = factor * jnp.dot(cotangent, weight.T, preferred_element_type=jnp.float32)
    gain_gradient = lax.optimization_barrier(jnp.sum(feature_gradient * normalized_input_wide, axis=0))
    normalized_gradient = lax.optimization_barrier((feature_gradient * gain_wide).astype(jnp.bfloat16)).astype(jnp.float32)
    inner_width = lax.optimization_barrier(jnp.mean(normalized_gradient * normalized_input_wide, axis=-1, keepdims=True))
    input_gradient = (inverse_deviation * (normalized_gradient - normalized_input_wide * inner_width)).astype(jnp.bfloat16)
    new_weight = (weight.astype(jnp.float32) - learn_rate * wgrad).astype(jnp.bfloat16)
    new_gain = (gain_wide - gain_rate * gain_gradient).astype(jnp.bfloat16)
    return (input_gradient, new_weight, new_gain)

def reference(inputs, cotangent, weight, gain, step):
    grouped_in = inputs.reshape(N_REP, -1, D)
    grouped_cot = cotangent.reshape(N_REP, -1, HQ)
    input_gradient, new_weight, new_gain = lax.map(one_replica, (grouped_in, grouped_cot, weight, gain))
    exponent = jnp.remainder(step[0].astype(jnp.int32), jnp.int32(LOG_REP)).astype(jnp.int32)
    offset = jnp.left_shift(jnp.int32(1), exponent)
    partner_weight = jnp.roll(new_weight, offset, axis=0)
    partner_gain = jnp.roll(new_gain, offset, axis=0)
    weight_out = ((new_weight.astype(jnp.float32) + partner_weight.astype(jnp.float32)) * 0.5).astype(jnp.bfloat16)
    gain_out = ((new_gain.astype(jnp.float32) + partner_gain.astype(jnp.float32)) * 0.5).astype(jnp.bfloat16)
    return (input_gradient.reshape(TOKENS, D), weight_out, gain_out)
```

```python
from functools import partial

import jax
import jax.numpy as jnp
from jax import lax
from jax.experimental import pallas as pl
from jax.experimental.pallas import tpu as pltpu
from jax.sharding import PartitionSpec as P

MESH = pl.DeviceIdType.MESH
F32 = jnp.float32
BF16 = jnp.bfloat16

epsilon = 1e-05
learn_rate = 0.5
gain_rate = 0.01

COLS = 2
RING = 8
PEERS = COLS * RING
CHUNKS = 2
PARTS = 2
CROSS = ((0, 1, -1, 2, -2, 3), (1, -1, 2, -2, 3, 0))


def tiles(width, step):
    return [(at, min(step, width - at)) for at in range(0, width, step)]


def column_of(row):
    n = row.shape[1]
    i = lax.broadcasted_iota(jnp.int32, (n, n), 0)
    j = lax.broadcasted_iota(jnp.int32, (n, n), 1)
    return jnp.sum(jnp.where(i == j, row, 0.0), axis=1, keepdims=True)


def row_of(column):
    n = column.shape[0]
    i = lax.broadcasted_iota(jnp.int32, (n, n), 0)
    j = lax.broadcasted_iota(jnp.int32, (n, n), 1)
    return jnp.sum(jnp.where(i == j, column, 0.0), axis=0, keepdims=True)


def body(
    offset,
    x_hbm, cot_hbm, w_hbm, gain_ref,
    ig_hbm, wout_hbm, gout_ref,
    cot, xin, xt, xc, w, acc, fg, gg, dxt, ret, nw, got, ng, gotg,
    local_sem, ag_send, ag_recv, x_send, x_recv, r_send, r_recv, g_send, g_recv,
):
    rows, width = xin.shape
    feat = xc.shape[1]
    half = cot.shape[3]
    factor = width ** (-0.5)

    reps = lax.axis_size("rep")
    rep = lax.axis_index("rep")
    me = lax.axis_index("fsdp")
    col = me // RING
    z = me % RING
    my_slot = 2 * z + col

    my_cot = [cot.at[h, z, pl.ds(pl.multiple_of(col * rows, rows), rows), :] for h in range(CHUNKS)]
    in_x = pltpu.make_async_copy(x_hbm, xin, local_sem.at[0])
    in_cot = [
        pltpu.make_async_copy(cot_hbm.at[:, pl.ds(h * half, half)], my_cot[h], local_sem.at[1 + h])
        for h in range(CHUNKS)
    ]
    in_w = [
        pltpu.make_async_copy(w_hbm.at[:, pl.ds(h * half, half)], w.at[h], local_sem.at[3 + h])
        for h in range(CHUNKS)
    ]
    in_cot[0].start()
    in_x.start()
    in_cot[1].start()
    in_w[0].start()
    in_w[1].start()

    barrier = pltpu.get_barrier_semaphore()
    greeted = PEERS - 1
    for k in range(1, PEERS):
        pl.semaphore_signal(
            barrier, inc=1, device_id=(rep, (me + k) % PEERS), device_id_type=MESH
        )
    if offset is not None:
        to_rep = (rep + offset) % reps
        from_rep = (rep + reps - offset) % reps
        for peer in (to_rep, from_rep):
            pl.semaphore_signal(barrier, inc=1, device_id=(peer, me), device_id_type=MESH)
        greeted += 2
    pl.semaphore_wait(barrier, greeted)

    def sign(h):
        return 1 - 2 * h

    def origin(h, d):
        return (z + 2 * RING - sign(h) * d) % RING

    def block(h, d, c):
        return cot.at[h, origin(h, d), pl.ds(pl.multiple_of(c * rows, rows), rows), :]

    def recv_index(h, d, c):
        return h * PEERS + 2 * origin(h, d) + c

    def ag_copy(h, d, other, way, number):
        c = (1 - col) if other else col
        if way == "x":
            target = (1 - col) * RING + z
        elif way == "lead":
            target = col * RING + (z + RING + sign(h)) % RING
        else:
            target = col * RING + (z + RING - sign(h)) % RING
        part = block(h, d, c)
        return pltpu.make_async_remote_copy(
            src_ref=part,
            dst_ref=part,
            send_sem=ag_send.at[number],
            recv_sem=ag_recv.at[recv_index(h, d, c)],
            device_id=(rep, target),
            device_id_type=MESH,
        )

    sent = []

    def send(h, d, other, way):
        key = (h, d, other, way)
        sent.append(key)
        ag_copy(h, d, other, way, len(sent) - 1).start()

    def arrived(h, d, c):
        part = block(h, d, c)
        pltpu.make_async_remote_copy(
            src_ref=part,
            dst_ref=part,
            send_sem=ag_send.at[0],
            recv_sem=ag_recv.at[recv_index(h, d, c)],
            device_id=(rep, (1 - col) * RING + z),
            device_id_type=MESH,
        ).wait_recv()

    def ring_start(h):
        if CROSS[h][0] == 0:
            send(h, 0, False, "x")
        send(h, 0, False, "lead")
        send(h, 0, False, "trail")

    def ring_step(h, k):
        arrived(h, k, col)
        if k <= 3:
            send(h, k, False, "lead")
            send(h, k, False, "x")
        if k <= 3:
            arrived(h, -k, col)
            if k <= 2:
                send(h, -k, False, "trail")
                send(h, -k, False, "x")
        if k == 3 and CROSS[h][0] != 0:
            send(h, 0, False, "x")

    in_cot[0].wait()
    ring_start(0)

    in_x.wait()
    lanes = 512 if width % 512 == 0 else 128

    def square(k, total):
        part = xin[:, pl.ds(pl.multiple_of(k * lanes, lanes), lanes)].astype(F32)
        part = part * part
        for at, size in tiles(lanes, 128):
            total = total + part[:, at : at + size]
        return total

    total = lax.fori_loop(0, width // lanes, square, jnp.zeros((rows, 128), F32))
    rstd = lax.rsqrt(jnp.sum(total, axis=1, keepdims=True) / width + epsilon)

    def normalize(k, carry):
        at = pl.multiple_of(k * 128, 128)
        part = (xin[:, pl.ds(at, 128)].astype(F32) * rstd).astype(BF16).astype(F32)
        xt[pl.ds(at, 128), :] = part.T.astype(BF16)
        return carry

    lax.fori_loop(0, width // 128, normalize, 0)

    def xt_rows(j):
        return pl.ds(pl.multiple_of(j * feat, 16), feat)

    def slot_of(j):
        return 2 * (j % RING) + j // RING

    def x_copy(k):
        j = (me + k) % PEERS
        return pltpu.make_async_remote_copy(
            src_ref=xt.at[xt_rows(j), :],
            dst_ref=xc.at[my_slot],
            send_sem=x_send.at[k],
            recv_sem=x_recv.at[my_slot],
            device_id=(rep, j),
            device_id_type=MESH,
        )

    def x_arrived(slot):
        pltpu.make_async_remote_copy(
            src_ref=xc.at[slot],
            dst_ref=xc.at[slot],
            send_sem=x_send.at[0],
            recv_sem=x_recv.at[slot],
            device_id=(rep, (1 - col) * RING + z),
            device_id_type=MESH,
        ).wait_recv()

    def start_x(k, carry):
        x_copy(k).start()
        return carry

    lax.fori_loop(1, PEERS, start_x, 0)
    own_x = pltpu.make_async_copy(xt.at[xt_rows(me), :], xc.at[my_slot], local_sem.at[5])
    own_x.start()
    gain = column_of(gain_ref[...].astype(F32))
    gg[...] = jnp.zeros_like(gg)
    own_x.wait()
    for copy in in_w:
        copy.wait()

    def g_copy(h, p):
        size = feat // PARTS
        return pltpu.make_async_remote_copy(
            src_ref=nw.at[h, pl.ds(p * size, size), :],
            dst_ref=got.at[h, pl.ds(p * size, size), :],
            send_sem=g_send.at[h * PARTS + p],
            recv_sem=g_recv.at[h * PARTS + p],
            device_id=(to_rep, me),
            device_id_type=MESH,
        )

    def finish_chunk(h):
        size = feat // PARTS
        for p in range(PARTS):
            part = pl.ds(p * size, size)
            for at, n in tiles(half, 256):
                old = w[h, part, pl.ds(at, n)].astype(F32)
                nw[h, part, pl.ds(at, n)] = (
                    old - learn_rate * (factor * acc[part, pl.ds(at, n)])
                ).astype(BF16)
            if offset is not None:
                g_copy(h, p).start()

    def step(u, carry):
        h = u // RING
        t = u % RING
        @pl.when(u == 0)
        def _():
            ring_step(0, 1)

        @pl.when(u == 1)
        def _():
            ring_step(0, 2)

        @pl.when(u == 2)
        def _():
            ring_step(0, 3)
            in_cot[1].wait()
            ring_start(1)

        @pl.when(u == 3)
        def _():
            ring_step(0, 4)

        @pl.when(u == 4)
        def _():
            ring_step(1, 1)

        @pl.when(u == 5)
        def _():
            ring_step(1, 2)

        @pl.when(u == 6)
        def _():
            ring_step(1, 3)

        @pl.when(u == 7)
        def _():
            ring_step(1, 4)

        tt = (t + h) % RING
        d = ((tt + 1) // 2) * (2 * (tt % 2) - 1)
        pair = (z + 2 * RING - (1 - 2 * h) * d) % RING
        arrived(h, d, 1 - col)

        for number, (ch, cd, way) in enumerate(
            ((0, -2, "trail"), (0, 3, "lead"), (1, -2, "trail"), (1, 3, "lead"))
        ):
            at = ch * RING + ((2 * cd - 1 if cd > 0 else -2 * cd) + RING - ch) % RING

            @pl.when(u == at)
            def _():
                send(ch, cd, True, way)

        @pl.when(h == 0)
        def _():
            x_arrived(2 * pair + (1 - col))

            @pl.when(t > 0)
            def _():
                x_arrived(2 * pair + col)

        @pl.when(t == 0)
        def _():
            acc[...] = jnp.zeros_like(acc)

        xh = jnp.concatenate([xc[2 * pair], xc[2 * pair + 1]], axis=1).astype(F32)
        xn = (xh * gain).astype(BF16)
        for at, n in tiles(half, 256):
            acc[:, pl.ds(at, n)] += jnp.dot(
                xn, cot[h, pair, :, pl.ds(at, n)], preferred_element_type=F32
            )
        feature = lax.dot_general(
            w[h], cot[h, pair], (((1,), (1,)), ((), ())), preferred_element_type=F32
        )

        @pl.when(h == 0)
        def _():
            fg[pair] = feature

        @pl.when(h == 1)
        def _():
            whole = factor * (fg[pair] + feature)
            prod = whole * jnp.concatenate([xc[2 * pair], xc[2 * pair + 1]], axis=1).astype(F32)
            gg[...] += prod[:, :rows] + prod[:, rows:]
            dx = (whole * gain).astype(BF16)
            dxt[2 * pair] = dx[:, :rows]
            dxt[2 * pair + 1] = dx[:, rows:]

        for ch in range(CHUNKS):

            @pl.when(u == ch * RING + RING - 1)
            def _():
                finish_chunk(ch)

        return carry

    lax.fori_loop(0, CHUNKS * RING, step, 0)

    def ret_rows(j):
        return pl.ds(pl.multiple_of(j * feat, 16), feat)

    def r_copy(k):
        j = (me + k) % PEERS
        return pltpu.make_async_remote_copy(
            src_ref=dxt.at[slot_of(j)],
            dst_ref=ret.at[ret_rows(me), :],
            send_sem=r_send.at[k],
            recv_sem=r_recv.at[me],
            device_id=(rep, j),
            device_id_type=MESH,
        )

    def r_arrived(j):
        pltpu.make_async_remote_copy(
            src_ref=dxt.at[0],
            dst_ref=ret.at[ret_rows(j), :],
            send_sem=r_send.at[0],
            recv_sem=r_recv.at[j],
            device_id=(rep, (1 - col) * RING + z),
            device_id_type=MESH,
        ).wait_recv()

    def start_r(k, carry):
        r_copy(k).start()
        return carry

    lax.fori_loop(1, PEERS, start_r, 0)
    own_r = pltpu.make_async_copy(dxt.at[my_slot], ret.at[ret_rows(me), :], local_sem.at[5])
    own_r.start()

    total_gain = jnp.sum(gg[...], axis=1, keepdims=True)
    new_gain = row_of((gain - gain_rate * total_gain).astype(BF16).astype(F32))
    if offset is None:
        gout_ref[...] = new_gain
        out_w = [
            pltpu.make_async_copy(nw.at[h], wout_hbm.at[:, pl.ds(h * half, half)], local_sem.at[1 + h])
            for h in range(CHUNKS)
        ]
        for copy in out_w:
            copy.start()
    else:
        ng[...] = jnp.zeros_like(ng)
        ng[0:1, 0:feat] = new_gain
        gain_copy = pltpu.make_async_remote_copy(
            src_ref=ng,
            dst_ref=gotg,
            send_sem=g_send.at[CHUNKS * PARTS],
            recv_sem=g_recv.at[CHUNKS * PARTS],
            device_id=(to_rep, me),
            device_id_type=MESH,
        )
        gain_copy.start()

    def part_of(j):
        def add(k, total):
            at = pl.multiple_of(j * feat + k * 32, 16)
            prod = ret[pl.ds(at, 32), :].astype(F32) * xt[pl.ds(at, 32), :].astype(F32)
            return total + (prod[0:8] + prod[8:16]) + (prod[16:24] + prod[24:32])

        return add

    own_r.wait()
    inner = lax.fori_loop(0, feat // 32, part_of(me), jnp.zeros((8, rows), F32))

    def add_return(k, inner):
        j = (me + k) % PEERS
        r_arrived(j)
        return lax.fori_loop(0, feat // 32, part_of(j), inner)

    inner = lax.fori_loop(1, PEERS, add_return, inner)
    mean = jnp.sum(inner, axis=0, keepdims=True) / width

    def finish(k, carry):
        at = pl.multiple_of(k * 128, 128)
        part = ret[pl.ds(at, 128), :].astype(F32) - xt[pl.ds(at, 128), :].astype(F32) * mean
        xin[:, pl.ds(at, 128)] = (part.T * rstd).astype(BF16)
        return carry

    lax.fori_loop(0, width // 128, finish, 0)
    out_x = pltpu.make_async_copy(xin, ig_hbm, local_sem.at[0])
    out_x.start()

    if offset is not None:
        out_w = []
        size = feat // PARTS
        for h in range(CHUNKS):
            for p in range(PARTS):
                g_copy(h, p).wait_recv()
                part = pl.ds(p * size, size)
                for at, n in tiles(half, 256):
                    got[h, part, pl.ds(at, n)] = (
                        (nw[h, part, pl.ds(at, n)].astype(F32) + got[h, part, pl.ds(at, n)].astype(F32))
                        * 0.5
                    ).astype(BF16)
                copy = pltpu.make_async_copy(
                    got.at[h, part, :],
                    wout_hbm.at[part, pl.ds(h * half, half)],
                    local_sem.at[1 + h * PARTS + p],
                )
                copy.start()
                out_w.append(copy)
        gain_copy.wait_recv()
        gout_ref[...] = (new_gain + gotg[0:1, 0:feat]) * 0.5
        for h in range(CHUNKS):
            for p in range(PARTS):
                g_copy(h, p).wait_send()
        gain_copy.wait_send()

    for number, (h, d, other, way) in enumerate(sent):
        ag_copy(h, d, other, way, number).wait_send()

    def drain(k, carry):
        x_copy(k).wait_send()
        r_copy(k).wait_send()
        return carry

    lax.fori_loop(1, PEERS, drain, 0)
    out_x.wait()
    for copy in out_w:
        copy.wait()


def run(offset, call_id, inputs, cotangent, weight, gain):
    rows, width = inputs.shape
    feat, proj = weight.shape
    half = proj // CHUNKS
    any_space = pl.BlockSpec(memory_space=pl.ANY)
    vmem = pl.BlockSpec(memory_space=pltpu.VMEM)
    dma = pltpu.SemaphoreType.DMA
    return pl.pallas_call(
        partial(body, offset),
        out_shape=(
            jax.ShapeDtypeStruct((rows, width), BF16),
            jax.ShapeDtypeStruct((feat, proj), BF16),
            jax.ShapeDtypeStruct((1, feat), F32),
        ),
        in_specs=[any_space, any_space, any_space, vmem],
        out_specs=(any_space, any_space, vmem),
        scratch_shapes=[
            pltpu.VMEM((CHUNKS, RING, COLS * rows, half), BF16),
            pltpu.VMEM((rows, width), BF16),
            pltpu.VMEM((width, rows), BF16),
            pltpu.VMEM((PEERS, feat, rows), BF16),
            pltpu.VMEM((CHUNKS, feat, half), BF16),
            pltpu.VMEM((feat, half), F32),
            pltpu.VMEM((RING, feat, COLS * rows), F32),
            pltpu.VMEM((feat, rows), F32),
            pltpu.VMEM((PEERS, feat, rows), BF16),
            pltpu.VMEM((width, rows), BF16),
            pltpu.VMEM((CHUNKS, feat, half), BF16),
            pltpu.VMEM((CHUNKS, feat, half), BF16),
            pltpu.VMEM((8, 512), F32),
            pltpu.VMEM((8, 512), F32),
            dma((8,)),
            dma((15 * CHUNKS,)),
            dma((CHUNKS * PEERS,)),
            dma((PEERS,)),
            dma((PEERS,)),
            dma((PEERS,)),
            dma((PEERS,)),
            dma((CHUNKS * PARTS + 1,)),
            dma((CHUNKS * PARTS + 1,)),
        ],
        compiler_params=pltpu.CompilerParams(
            collective_id=call_id, has_side_effects=True, vmem_limit_bytes=56 * 1024 * 1024
        ),
    )(inputs, cotangent, weight, gain)


def per_device(inputs, cotangent, weight, gain, step):
    levels = lax.axis_size("rep").bit_length() - 1
    exponent = jnp.remainder(step[0], levels)
    branches = [partial(run, 1 << level, 1 + level) for level in range(levels)]
    input_gradient, weight_out, gain_out = lax.switch(
        exponent, branches, inputs, cotangent, weight[0], gain
    )
    return (input_gradient, weight_out[None], gain_out.astype(BF16))


def solution(mesh):
    in_specs = (
        P(("rep", "fsdp"), None),
        P(("rep", "fsdp"), None),
        P("rep", "fsdp", None),
        P("rep", "fsdp"),
        P(),
    )
    out_specs = (P(("rep", "fsdp"), None), P("rep", "fsdp", None), P("rep", "fsdp"))
    return jax.shard_map(
        per_device, mesh=mesh, in_specs=in_specs, out_specs=out_specs, check_vma=False
    )
```

```python
from functools import partial

import jax
import jax.numpy as jnp
from jax import lax
from jax.experimental import pallas as pl
from jax.experimental.pallas import tpu as pltpu
from jax.sharding import PartitionSpec as P

MESH = pl.DeviceIdType.MESH
F32 = jnp.float32
BF16 = jnp.bfloat16

epsilon = 1e-05
learn_rate = 0.5
gain_rate = 0.01

COLS = 2
RING = 8
CHUNKS = 4
PARTS = 2
PAIRS = RING // 2


def tiles(width, step):
    return [(at, min(step, width - at)) for at in range(0, width, step)]


def column_of(row):
    n = row.shape[1]
    i = lax.broadcasted_iota(jnp.int32, (n, n), 0)
    j = lax.broadcasted_iota(jnp.int32, (n, n), 1)
    return jnp.sum(jnp.where(i == j, row, 0.0), axis=1, keepdims=True)


def row_of(column):
    n = column.shape[0]
    i = lax.broadcasted_iota(jnp.int32, (n, n), 0)
    j = lax.broadcasted_iota(jnp.int32, (n, n), 1)
    return jnp.sum(jnp.where(i == j, column, 0.0), axis=0, keepdims=True)


def chunk_sizes(width):
    blocks = width // 128
    return [128 * (blocks // CHUNKS + (h < blocks % CHUNKS)) for h in range(CHUNKS)]


def body(
    offset,
    x_hbm, cot_hbm, w_hbm, gain_ref,
    ig_hbm, wout_hbm, gout_ref,
    cot, w, acc, pw, gp, nw, got,
    xin, xt, xc, xn, fg, gg, gb, dxt, ret, gbuf, gsum, ng,
    local_sem, ag_send, ag_recv, w_send, w_recv, x_send, x_recv, p_send, p_recv,
    r_send, r_recv, g_send, g_recv, s_send, s_recv,
):
    rows, width = xin.shape
    feat = xc.shape[2]
    sizes = [c.shape[2] for c in cot]
    starts = [sum(sizes[:h]) for h in range(CHUNKS)]
    factor = width ** (-0.5)
    part_rows = feat // PARTS

    reps = lax.axis_size("rep")
    rep = lax.axis_index("rep")
    me = lax.axis_index("fsdp")
    col = me // RING
    z = me % RING
    across = (rep, (1 - col) * RING + z)
    to_rep = (rep + offset) % reps
    from_rep = (rep + reps - offset) % reps

    def remote(src, dst, send_sem, recv_sem, device):
        return pltpu.make_async_remote_copy(
            src_ref=src, dst_ref=dst, send_sem=send_sem, recv_sem=recv_sem,
            device_id=device, device_id_type=MESH,
        )

    barrier = pltpu.get_barrier_semaphore()
    for k in range(1, RING):
        pl.semaphore_signal(
            barrier, inc=1, device_id=(rep, col * RING + (z + k) % RING), device_id_type=MESH
        )
    for device in (across, (to_rep, me), (from_rep, me)):
        pl.semaphore_signal(barrier, inc=1, device_id=device, device_id_type=MESH)

    in_cot = [
        pltpu.make_async_copy(cot_hbm.at[:, pl.ds(starts[h], sizes[h])], cot[h].at[z], local_sem.at[h])
        for h in range(CHUNKS)
    ]
    in_w = [
        pltpu.make_async_copy(
            w_hbm.at[:, pl.ds(starts[h], sizes[h])], w[h].at[col], local_sem.at[CHUNKS + h]
        )
        for h in range(CHUNKS)
    ]
    in_x = pltpu.make_async_copy(x_hbm, xin, local_sem.at[2 * CHUNKS])
    in_cot[0].start()
    in_x.start()
    for h in range(CHUNKS):
        in_w[h].start()
    for h in range(1, CHUNKS):
        in_cot[h].start()
    gbuf[col] = jnp.zeros(gbuf.shape[1:], F32)
    gbuf[col, 0:1, 0:feat] = gain_ref[...].astype(F32)

    pl.semaphore_wait(barrier, RING + 2)

    def sign(h):
        return 1 - 2 * (h % 2)

    def origin(h, d):
        return (z + 2 * RING - sign(h) * d) % RING

    def ag_copy(h, d, way, number):
        step = sign(h) if way == "lead" else -sign(h)
        block = cot[h].at[origin(h, d)]
        return remote(
            block, block, ag_send.at[number], ag_recv.at[h * RING + origin(h, d)],
            (rep, col * RING + (z + RING + step) % RING),
        )

    sent = []

    def send(h, d, way):
        sent.append((h, d, way))
        ag_copy(h, d, way, len(sent) - 1).start()

    def arrived(h, d):
        block = cot[h].at[origin(h, d)]
        remote(
            block, block, ag_send.at[0], ag_recv.at[h * RING + origin(h, d)], across
        ).wait_recv()

    def ring_start(h):
        in_cot[h].wait()
        send(h, 0, "lead")
        send(h, 0, "trail")

    def ring_step(h, k):
        arrived(h, k)
        if k <= 3:
            send(h, k, "lead")
            arrived(h, -k)
        if k <= 2:
            send(h, -k, "trail")

    ring_start(0)

    in_x.wait()
    lanes = 512 if width % 512 == 0 else 128

    def square(k, total):
        part = xin[:, pl.ds(pl.multiple_of(k * lanes, lanes), lanes)].astype(F32)
        part = part * part
        for at, size in tiles(lanes, 128):
            total = total + part[:, at : at + size]
        return total

    total = lax.fori_loop(0, width // lanes, square, jnp.zeros((rows, 128), F32))
    rstd = lax.rsqrt(jnp.sum(total, axis=1, keepdims=True) / width + epsilon)
    side = width // COLS // 128

    def normalize(k, carry):
        for c in range(COLS):
            at = pl.multiple_of((c * side + k) * 128, 128)
            part = (xin[:, pl.ds(at, 128)].astype(F32) * rstd).astype(BF16).astype(F32)
            xt[c, pl.ds(pl.multiple_of(k * 128, 128), 128), :] = part.T.astype(BF16)
        return carry

    lax.fori_loop(0, side, normalize, 0)

    def feat_rows(j):
        return pl.ds(pl.multiple_of(j * feat, 16), feat)

    def x_copy(k):
        j = (z + k) % RING
        return remote(
            xt.at[:, feat_rows(j), :], xc.at[z], x_send.at[k], x_recv.at[z], (rep, col * RING + j)
        )

    def x_arrived(j):
        remote(xc.at[j], xc.at[j], x_send.at[0], x_recv.at[j], across).wait_recv()

    def start_x(k, carry):
        x_copy(k).start()
        return carry

    lax.fori_loop(1, RING, start_x, 0)
    own_x = pltpu.make_async_copy(xt.at[:, feat_rows(z), :], xc.at[z], local_sem.at[2 * CHUNKS])
    own_x.start()

    gain_copy = remote(gbuf.at[col], gbuf.at[col], s_send.at[0], s_recv.at[0], across)
    gain_copy.start()

    def w_copy(h):
        return remote(w[h].at[col], w[h].at[col], w_send.at[h], w_recv.at[h], across)

    for h in range(CHUNKS):
        in_w[h].wait()
        w_copy(h).start()

    gg[...] = jnp.zeros_like(gg)
    own_x.wait()

    def rows_of(p):
        return pl.ds(p * part_rows, part_rows)

    def p_copy(h, p):
        number = h * PARTS + p
        return remote(
            pw[h].at[rows_of(p), :], gp[h].at[rows_of(p), :], p_send.at[number], p_recv.at[number], across
        )

    def g_copy(h, p):
        number = h * PARTS + p
        return remote(
            nw[h].at[rows_of(p), :], got[h].at[rows_of(p), :], g_send.at[number], g_recv.at[number],
            (to_rep, me),
        )

    def hand_over(h):
        for p in range(PARTS):
            for at, n in tiles(sizes[h], 256):
                pw[h][rows_of(p), pl.ds(at, n)] = acc[h][1 - col, rows_of(p), pl.ds(at, n)].astype(BF16)
            p_copy(h, p).start()

    def update(h):
        for p in range(PARTS):
            p_copy(h, p).wait_recv()
            for at, n in tiles(sizes[h], 256):
                whole = acc[h][col, rows_of(p), pl.ds(at, n)] + gp[h][rows_of(p), pl.ds(at, n)].astype(F32)
                old = w[h][col, rows_of(p), pl.ds(at, n)].astype(F32)
                nw[h][rows_of(p), pl.ds(at, n)] = (old - learn_rate * (factor * whole)).astype(BF16)
            g_copy(h, p).start()

    out_w = []

    def average(h):
        for p in range(PARTS):
            g_copy(h, p).wait_recv()
            for at, n in tiles(sizes[h], 256):
                both = nw[h][rows_of(p), pl.ds(at, n)].astype(F32) + got[h][rows_of(p), pl.ds(at, n)].astype(F32)
                gp[h][rows_of(p), pl.ds(at, n)] = (both * 0.5).astype(BF16)
            copy = pltpu.make_async_copy(
                gp[h].at[rows_of(p), :],
                wout_hbm.at[rows_of(p), pl.ds(starts[h], sizes[h])],
                local_sem.at[2 * CHUNKS + 1 + h * PARTS + p],
            )
            copy.start()
            out_w.append(copy)

    def r_copy(j):
        return remote(
            dxt.at[j], ret.at[:, feat_rows(z), :], r_send.at[j], r_recv.at[z], (rep, col * RING + j)
        )

    own_r = pltpu.make_async_copy(dxt.at[z], ret.at[:, feat_rows(z), :], local_sem.at[2 * CHUNKS])

    def step(h, events, t, carry):
        for at, event in events:
            pl.when(t == at)(event)
        far = sign(h) * (t + 1)
        near = -sign(h) * ((t + 1) % PAIRS)
        a = (z + 2 * RING - far) % RING
        b = (z + 2 * RING - near) % RING
        if h == 0:
            x_arrived(a)

            @pl.when(t < PAIRS - 1)
            def _():
                x_arrived(b)

        @pl.when(t == 0)
        def _():
            acc[h][...] = jnp.zeros_like(acc[h])

        for c in range(COLS):
            if h == 0:
                for j in (a, b):
                    xn[j, c] = (xc[j, c].astype(F32) * gb[c]).astype(BF16)
            lhs = jnp.concatenate([xn[a, c], xn[b, c]], axis=1)
            for at, n in tiles(sizes[h], 256):
                ct = jnp.concatenate([cot[h][a, :, pl.ds(at, n)], cot[h][b, :, pl.ds(at, n)]], axis=0)
                acc[h][c, :, pl.ds(at, n)] += jnp.dot(lhs, ct, preferred_element_type=F32)

        @pl.when(t == 0)
        def _():
            w_copy(h).wait_recv()

        ct = jnp.concatenate([cot[h][a], cot[h][b]], axis=0)
        for c in range(COLS):
            feature = lax.dot_general(
                w[h][c], ct, (((1,), (1,)), ((), ())), preferred_element_type=F32
            )
            if h == 0:
                fg[a, c] = feature[:, :rows]
                fg[b, c] = feature[:, rows:]
            elif h < CHUNKS - 1:
                fg[a, c] += feature[:, :rows]
                fg[b, c] += feature[:, rows:]
            else:
                for j, part in ((a, feature[:, :rows]), (b, feature[:, rows:])):
                    whole = factor * (fg[j, c] + part)
                    gg[c] += whole * xc[j, c].astype(F32)
                    dxt[j, c] = (whole * gb[c]).astype(BF16)
        if h == CHUNKS - 1:
            r_copy(a).start()

            @pl.when(t < PAIRS - 1)
            def _():
                r_copy(b).start()

        return carry

    def compute(h, *events):
        lax.fori_loop(0, PAIRS, partial(step, h, events), 0)

    ring_step(0, 1)
    ring_step(0, 2)
    ring_step(0, 3)
    ring_start(1)
    ring_step(0, 4)
    gain_copy.wait_recv()
    for c in range(COLS):
        gb[c] = jnp.broadcast_to(column_of(gbuf[c, 0:1, 0:feat]), gb.shape[1:])

    def turn_2():
        ring_start(2)
        ring_step(1, 2)

    compute(0, (1, lambda: ring_step(1, 1)), (3, turn_2))
    hand_over(0)
    ring_step(1, 3)
    ring_start(3)
    ring_step(2, 1)
    ring_step(1, 4)

    def turn_3():
        ring_step(3, 1)
        ring_step(2, 2)

    compute(1, (2, turn_3))
    hand_over(1)
    update(0)
    ring_step(3, 2)
    ring_step(2, 3)
    ring_step(2, 4)
    compute(2, (2, lambda: ring_step(3, 3)))
    hand_over(2)
    update(1)
    compute(3, (3, lambda: ring_step(3, 4)))
    own_r.start()
    hand_over(3)

    gsum[0] = jnp.zeros(gsum.shape[1:], F32)
    gsum[0, 0:1, 0:feat] = row_of(jnp.sum(gg[1 - col], axis=1, keepdims=True))
    sum_copy = remote(gsum.at[0], gsum.at[1], s_send.at[1], s_recv.at[1], across)
    sum_copy.start()
    own_sum = row_of(jnp.sum(gg[col], axis=1, keepdims=True))
    sum_copy.wait_recv()
    total_gain = own_sum + gsum[1, 0:1, 0:feat]
    new_gain = (gbuf[col, 0:1, 0:feat] - gain_rate * total_gain).astype(BF16).astype(F32)
    ng[0] = jnp.zeros(ng.shape[1:], F32)
    ng[0, 0:1, 0:feat] = new_gain
    new_gain_copy = remote(ng.at[0], ng.at[1], s_send.at[2], s_recv.at[2], (to_rep, me))
    new_gain_copy.start()
    update(2)
    update(3)
    average(0)
    average(1)

    def add_part(j, inner):
        def add(k, inner):
            for c in range(COLS):
                at = pl.ds(pl.multiple_of(j * feat + k * 32, 16), 32)
                prod = ret[c, at, :].astype(F32) * xt[c, at, :].astype(F32)
                inner = inner + ((prod[0:8] + prod[8:16]) + (prod[16:24] + prod[24:32]))
            return inner

        return lax.fori_loop(0, feat // 32, add, inner)

    own_r.wait()
    inner = add_part(z, jnp.zeros((8, rows), F32))

    def add_return(k, inner):
        j = (z + k) % RING
        remote(dxt.at[0], ret.at[:, feat_rows(j), :], r_send.at[0], r_recv.at[j], across).wait_recv()
        return add_part(j, inner)

    inner = lax.fori_loop(1, RING, add_return, inner)
    mean = jnp.sum(inner, axis=0, keepdims=True) / width

    def finish(k, carry):
        for c in range(COLS):
            at = pl.ds(pl.multiple_of(k * 128, 128), 128)
            part = ret[c, at, :].astype(F32) - xt[c, at, :].astype(F32) * mean
            xin[:, pl.ds(pl.multiple_of((c * side + k) * 128, 128), 128)] = (part.T * rstd).astype(BF16)
        return carry

    lax.fori_loop(0, side, finish, 0)
    out_x = pltpu.make_async_copy(xin, ig_hbm, local_sem.at[2 * CHUNKS])
    out_x.start()
    average(2)
    average(3)
    new_gain_copy.wait_recv()
    gout_ref[...] = (new_gain + ng[1, 0:1, 0:feat]) * 0.5

    for number, (h, d, way) in enumerate(sent):
        ag_copy(h, d, way, number).wait_send()
    for h in range(CHUNKS):
        w_copy(h).wait_send()
        for p in range(PARTS):
            p_copy(h, p).wait_send()
            g_copy(h, p).wait_send()
    for copy in (gain_copy, sum_copy, new_gain_copy):
        copy.wait_send()

    def drain(k, carry):
        x_copy(k).wait_send()
        r_copy((z + k) % RING).wait_send()
        return carry

    lax.fori_loop(1, RING, drain, 0)
    out_x.wait()
    for copy in out_w:
        copy.wait()


def run(offset, call_id, inputs, cotangent, weight, gain):
    rows, width = inputs.shape
    feat, proj = weight.shape
    sizes = chunk_sizes(proj)
    any_space = pl.BlockSpec(memory_space=pl.ANY)
    vmem = pl.BlockSpec(memory_space=pltpu.VMEM)
    dma = pltpu.SemaphoreType.DMA

    def chunks(shape, dtype):
        return [pltpu.VMEM((*shape, n), dtype) for n in sizes]

    side = (COLS, width // COLS, rows)
    return pl.pallas_call(
        partial(body, offset),
        out_shape=(
            jax.ShapeDtypeStruct((rows, width), BF16),
            jax.ShapeDtypeStruct((feat, proj), BF16),
            jax.ShapeDtypeStruct((1, feat), F32),
        ),
        in_specs=[any_space, any_space, any_space, vmem],
        out_specs=(any_space, any_space, vmem),
        scratch_shapes=[
            chunks((RING, rows), BF16),
            chunks((COLS, feat), BF16),
            chunks((COLS, feat), F32),
            chunks((feat,), BF16),
            chunks((feat,), BF16),
            chunks((feat,), BF16),
            chunks((feat,), BF16),
            pltpu.VMEM((rows, width), BF16),
            pltpu.VMEM(side, BF16),
            pltpu.VMEM((RING, COLS, feat, rows), BF16),
            pltpu.VMEM((RING, COLS, feat, rows), BF16),
            pltpu.VMEM((RING, COLS, feat, rows), F32),
            pltpu.VMEM((COLS, feat, rows), F32),
            pltpu.VMEM((COLS, feat, 128), F32),
            pltpu.VMEM((RING, COLS, feat, rows), BF16),
            pltpu.VMEM(side, BF16),
            pltpu.VMEM((COLS, 8, 512), F32),
            pltpu.VMEM((2, 8, 512), F32),
            pltpu.VMEM((2, 8, 512), F32),
            dma((2 * CHUNKS + 1 + CHUNKS * PARTS,)),
            dma((7 * CHUNKS,)),
            dma((RING * CHUNKS,)),
            dma((CHUNKS,)),
            dma((CHUNKS,)),
            dma((RING,)),
            dma((RING,)),
            dma((CHUNKS * PARTS,)),
            dma((CHUNKS * PARTS,)),
            dma((RING,)),
            dma((RING,)),
            dma((CHUNKS * PARTS,)),
            dma((CHUNKS * PARTS,)),
            dma((3,)),
            dma((3,)),
        ],
        compiler_params=pltpu.CompilerParams(
            collective_id=call_id, has_side_effects=True, vmem_limit_bytes=58 * 1024 * 1024
        ),
    )(inputs, cotangent, weight, gain)


def per_device(inputs, cotangent, weight, gain, step):
    levels = lax.axis_size("rep").bit_length() - 1
    exponent = jnp.remainder(step[0], levels)
    branches = [partial(run, 1 << level, 1 + level) for level in range(levels)]
    input_gradient, weight_out, gain_out = lax.switch(
        exponent, branches, inputs, cotangent, weight[0], gain
    )
    return (input_gradient, weight_out[None], gain_out.astype(BF16))


def solution(mesh):
    in_specs = (
        P(("rep", "fsdp"), None),
        P(("rep", "fsdp"), None),
        P("rep", "fsdp", None),
        P("rep", "fsdp"),
        P(),
    )
    out_specs = (P(("rep", "fsdp"), None), P("rep", "fsdp", None), P("rep", "fsdp"))
    return jax.shard_map(
        per_device, mesh=mesh, in_specs=in_specs, out_specs=out_specs, check_vma=False
    )
```

```python
from functools import partial

import jax
import jax.numpy as jnp
from jax import lax
from jax.experimental import pallas as pl
from jax.experimental.pallas import tpu as pltpu
from jax.sharding import PartitionSpec as P

MESH = pl.DeviceIdType.MESH
F32 = jnp.float32
BF16 = jnp.bfloat16

epsilon = 1e-05
learn_rate = 0.5
gain_rate = 0.01

COLS = 2
RING = 8
CHUNKS = 4
PARTS = 2
PAIRS = RING // 2


def tiles(width, step):
    return [(at, min(step, width - at)) for at in range(0, width, step)]


def column_of(row):
    n = row.shape[1]
    i = lax.broadcasted_iota(jnp.int32, (n, n), 0)
    j = lax.broadcasted_iota(jnp.int32, (n, n), 1)
    return jnp.sum(jnp.where(i == j, row, 0.0), axis=1, keepdims=True)


def row_of(column):
    n = column.shape[0]
    i = lax.broadcasted_iota(jnp.int32, (n, n), 0)
    j = lax.broadcasted_iota(jnp.int32, (n, n), 1)
    return jnp.sum(jnp.where(i == j, column, 0.0), axis=0, keepdims=True)


def chunk_sizes(width):
    blocks = width // 128
    return [128 * (blocks // CHUNKS + (h < blocks % CHUNKS)) for h in range(CHUNKS)]


def body(
    offset,
    x_hbm, cot_hbm, w_hbm, gain_ref,
    ig_hbm, wout_hbm, gout_ref,
    cot, w, acc, pw, gp, nw, got,
    xin, xt, xc, xn, fg, gg, gb, dxt, ret, gbuf, gsum, ng,
    local_sem, ag_send, ag_recv, w_send, w_recv, x_send, x_recv, p_send, p_recv,
    r_send, r_recv, g_send, g_recv, s_send, s_recv,
):
    rows, width = xin.shape
    feat = xc.shape[2]
    sizes = [c.shape[2] for c in cot]
    starts = [sum(sizes[:h]) for h in range(CHUNKS)]
    factor = width ** (-0.5)
    part_rows = feat // PARTS

    reps = lax.axis_size("rep")
    rep = lax.axis_index("rep")
    me = lax.axis_index("fsdp")
    col = me // RING
    z = me % RING
    across = (rep, (1 - col) * RING + z)
    to_rep = (rep + offset) % reps
    from_rep = (rep + reps - offset) % reps

    def remote(src, dst, send_sem, recv_sem, device):
        return pltpu.make_async_remote_copy(
            src_ref=src, dst_ref=dst, send_sem=send_sem, recv_sem=recv_sem,
            device_id=device, device_id_type=MESH,
        )

    barrier = pltpu.get_barrier_semaphore()
    for k in range(1, RING):
        pl.semaphore_signal(
            barrier, inc=1, device_id=(rep, col * RING + (z + k) % RING), device_id_type=MESH
        )
    for device in (across, (to_rep, me), (from_rep, me)):
        pl.semaphore_signal(barrier, inc=1, device_id=device, device_id_type=MESH)

    in_cot = [
        pltpu.make_async_copy(cot_hbm.at[:, pl.ds(starts[h], sizes[h])], cot[h].at[z], local_sem.at[h])
        for h in range(CHUNKS)
    ]
    in_w = [
        pltpu.make_async_copy(
            w_hbm.at[:, pl.ds(starts[h], sizes[h])], w[h].at[col], local_sem.at[CHUNKS + h]
        )
        for h in range(CHUNKS)
    ]
    in_x = pltpu.make_async_copy(x_hbm, xin, local_sem.at[2 * CHUNKS])
    in_cot[0].start()
    in_x.start()
    for h in range(CHUNKS):
        in_w[h].start()
    for h in range(1, CHUNKS):
        in_cot[h].start()
    gbuf[col] = jnp.zeros(gbuf.shape[1:], F32)
    gbuf[col, 0:1, 0:feat] = gain_ref[...].astype(F32)

    pl.semaphore_wait(barrier, RING + 2)

    def sign(p):
        return 1 - 2 * p

    def origin(p, d):
        return (z + 2 * RING - sign(p) * d) % RING

    def half_block(h, d, p):
        return cot[h].at[origin(p, d), pl.ds(p * (rows // 2), rows // 2), :]

    def recv_of(h, d, p):
        return ag_recv.at[(h * 2 + p) * RING + origin(p, d)]

    def ag_copy(h, d, p, way, number):
        step = sign(p) if way == "lead" else -sign(p)
        return remote(
            half_block(h, d, p), half_block(h, d, p), ag_send.at[number], recv_of(h, d, p),
            (rep, col * RING + (z + RING + step) % RING),
        )

    sent = []

    def send(h, d, p, way):
        sent.append((h, d, p, way))
        ag_copy(h, d, p, way, len(sent) - 1).start()

    def arrived(h, d, p):
        remote(
            half_block(h, d, p), half_block(h, d, p), ag_send.at[0], recv_of(h, d, p), across
        ).wait_recv()

    def ring_start(h):
        in_cot[h].wait()
        for way in ("lead", "trail"):
            for p in range(2):
                send(h, 0, p, way)

    def ring_step(h, k):
        for p in range(2):
            arrived(h, k, p)
            if k <= 3:
                send(h, k, p, "lead")
        if k <= 3:
            for p in range(2):
                arrived(h, -k, p)
                if k <= 2:
                    send(h, -k, p, "trail")

    ring_start(0)

    in_x.wait()
    lanes = 512 if width % 512 == 0 else 128

    def square(k, total):
        part = xin[:, pl.ds(pl.multiple_of(k * lanes, lanes), lanes)].astype(F32)
        part = part * part
        for at, size in tiles(lanes, 128):
            total = total + part[:, at : at + size]
        return total

    total = lax.fori_loop(0, width // lanes, square, jnp.zeros((rows, 128), F32))
    rstd = lax.rsqrt(jnp.sum(total, axis=1, keepdims=True) / width + epsilon)
    side = width // COLS // 128

    def normalize(k, carry):
        for c in range(COLS):
            at = pl.multiple_of((c * side + k) * 128, 128)
            part = (xin[:, pl.ds(at, 128)].astype(F32) * rstd).astype(BF16).astype(F32)
            xt[c, pl.ds(pl.multiple_of(k * 128, 128), 128), :] = part.T.astype(BF16)
        return carry

    lax.fori_loop(0, side, normalize, 0)

    def feat_rows(j):
        return pl.ds(pl.multiple_of(j * feat, 16), feat)

    def x_copy(k):
        j = (z + k) % RING
        return remote(
            xt.at[:, feat_rows(j), :], xc.at[z], x_send.at[k], x_recv.at[z], (rep, col * RING + j)
        )

    def x_arrived(j):
        remote(xc.at[j], xc.at[j], x_send.at[0], x_recv.at[j], across).wait_recv()

    def start_x(k, carry):
        x_copy(k).start()
        return carry

    lax.fori_loop(1, RING, start_x, 0)
    own_x = pltpu.make_async_copy(xt.at[:, feat_rows(z), :], xc.at[z], local_sem.at[2 * CHUNKS])
    own_x.start()

    gain_copy = remote(gbuf.at[col], gbuf.at[col], s_send.at[0], s_recv.at[0], across)
    gain_copy.start()

    def w_copy(h):
        return remote(w[h].at[col], w[h].at[col], w_send.at[h], w_recv.at[h], across)

    for h in range(CHUNKS):
        in_w[h].wait()
        w_copy(h).start()

    gg[...] = jnp.zeros_like(gg)
    own_x.wait()

    def rows_of(p):
        return pl.ds(p * part_rows, part_rows)

    def p_copy(h, p):
        number = h * PARTS + p
        return remote(
            pw[h].at[rows_of(p), :], gp[h].at[rows_of(p), :], p_send.at[number], p_recv.at[number], across
        )

    def g_copy(h, p):
        number = h * PARTS + p
        return remote(
            nw[h].at[rows_of(p), :], got[h].at[rows_of(p), :], g_send.at[number], g_recv.at[number],
            (to_rep, me),
        )

    def hand_over(h):
        for p in range(PARTS):
            for at, n in tiles(sizes[h], 256):
                pw[h][rows_of(p), pl.ds(at, n)] = acc[h][1 - col, rows_of(p), pl.ds(at, n)].astype(BF16)
            p_copy(h, p).start()

    def update(h):
        for p in range(PARTS):
            p_copy(h, p).wait_recv()
            for at, n in tiles(sizes[h], 256):
                whole = acc[h][col, rows_of(p), pl.ds(at, n)] + gp[h][rows_of(p), pl.ds(at, n)].astype(F32)
                old = w[h][col, rows_of(p), pl.ds(at, n)].astype(F32)
                nw[h][rows_of(p), pl.ds(at, n)] = (old - learn_rate * (factor * whole)).astype(BF16)
            g_copy(h, p).start()

    out_w = []

    def average(h):
        for p in range(PARTS):
            g_copy(h, p).wait_recv()
            for at, n in tiles(sizes[h], 256):
                both = nw[h][rows_of(p), pl.ds(at, n)].astype(F32) + got[h][rows_of(p), pl.ds(at, n)].astype(F32)
                gp[h][rows_of(p), pl.ds(at, n)] = (both * 0.5).astype(BF16)
            copy = pltpu.make_async_copy(
                gp[h].at[rows_of(p), :],
                wout_hbm.at[rows_of(p), pl.ds(starts[h], sizes[h])],
                local_sem.at[2 * CHUNKS + 1 + h * PARTS + p],
            )
            copy.start()
            out_w.append(copy)

    def r_copy(j):
        return remote(
            dxt.at[j], ret.at[:, feat_rows(z), :], r_send.at[j], r_recv.at[z], (rep, col * RING + j)
        )

    own_r = pltpu.make_async_copy(dxt.at[z], ret.at[:, feat_rows(z), :], local_sem.at[2 * CHUNKS])

    def pair_of(t):
        return (z + RING - (t + 1)) % RING, (z + (t + 1) % PAIRS) % RING

    def weight_step(h, events, t, carry):
        for at, event in events:
            pl.when(t == at)(event)
        a, b = pair_of(t)
        if h == 0:
            x_arrived(a)

            @pl.when(t < PAIRS - 1)
            def _():
                x_arrived(b)

        @pl.when(t == 0)
        def _():
            acc[h][...] = jnp.zeros_like(acc[h])

        for c in range(COLS):
            if h == 0:
                for j in (a, b):
                    xn[j, c] = (xc[j, c].astype(F32) * gb[c]).astype(BF16)
            lhs = jnp.concatenate([xn[a, c], xn[b, c]], axis=1)
            for at, n in tiles(sizes[h], 256):
                ct = jnp.concatenate([cot[h][a, :, pl.ds(at, n)], cot[h][b, :, pl.ds(at, n)]], axis=0)
                acc[h][c, :, pl.ds(at, n)] += jnp.dot(lhs, ct, preferred_element_type=F32)
        return carry

    def feature_step(h, t, carry):
        a, b = pair_of(t)
        ct = jnp.concatenate([cot[h][a], cot[h][b]], axis=0)
        for c in range(COLS):
            feature = lax.dot_general(
                w[h][c], ct, (((1,), (1,)), ((), ())), preferred_element_type=F32
            )
            if h == 0:
                fg[a, c] = feature[:, :rows]
                fg[b, c] = feature[:, rows:]
            elif h < CHUNKS - 1:
                fg[a, c] += feature[:, :rows]
                fg[b, c] += feature[:, rows:]
            else:
                for j, part in ((a, feature[:, :rows]), (b, feature[:, rows:])):
                    whole = factor * (fg[j, c] + part)
                    gg[c] += whole * xc[j, c].astype(F32)
                    dxt[j, c] = (whole * gb[c]).astype(BF16)
        if h == CHUNKS - 1:
            r_copy(a).start()

            @pl.when(t < PAIRS - 1)
            def _():
                r_copy(b).start()

        return carry

    def weight_sums(h, *events):
        lax.fori_loop(0, PAIRS, partial(weight_step, h, events), 0)

    def features(h):
        w_copy(h).wait_recv()
        lax.fori_loop(0, PAIRS, partial(feature_step, h), 0)

    ring_step(0, 1)
    ring_step(0, 2)
    ring_step(0, 3)
    ring_start(1)
    ring_step(0, 4)
    gain_copy.wait_recv()
    for c in range(COLS):
        gb[c] = jnp.broadcast_to(column_of(gbuf[c, 0:1, 0:feat]), gb.shape[1:])

    def turn_2():
        ring_start(2)
        ring_step(1, 2)

    weight_sums(0, (1, lambda: ring_step(1, 1)), (3, turn_2))
    hand_over(0)
    ring_step(1, 3)
    ring_start(3)
    ring_step(2, 1)
    ring_step(1, 4)
    weight_sums(1, (2, lambda: ring_step(2, 2)))
    hand_over(1)
    ring_step(3, 1)
    update(0)
    ring_step(2, 3)
    features(0)
    ring_step(3, 2)
    ring_step(2, 4)
    weight_sums(2)
    hand_over(2)
    ring_step(3, 3)
    update(1)
    features(1)
    features(2)
    w_copy(3).wait_recv()

    def last_step(t, carry):
        weight_step(3, (), t, 0)
        feature_step(3, t, 0)
        return carry

    lax.fori_loop(0, PAIRS - 1, last_step, 0)
    ring_step(3, 4)
    feature_step(3, jnp.int32(PAIRS - 1), 0)
    own_r.start()
    weight_step(3, (), jnp.int32(PAIRS - 1), 0)
    hand_over(3)
    update(2)

    gsum[0] = jnp.zeros(gsum.shape[1:], F32)
    gsum[0, 0:1, 0:feat] = row_of(jnp.sum(gg[1 - col], axis=1, keepdims=True))
    sum_copy = remote(gsum.at[0], gsum.at[1], s_send.at[1], s_recv.at[1], across)
    sum_copy.start()
    own_sum = row_of(jnp.sum(gg[col], axis=1, keepdims=True))
    sum_copy.wait_recv()
    total_gain = own_sum + gsum[1, 0:1, 0:feat]
    new_gain = (gbuf[col, 0:1, 0:feat] - gain_rate * total_gain).astype(BF16).astype(F32)
    ng[0] = jnp.zeros(ng.shape[1:], F32)
    ng[0, 0:1, 0:feat] = new_gain
    new_gain_copy = remote(ng.at[0], ng.at[1], s_send.at[2], s_recv.at[2], (to_rep, me))
    new_gain_copy.start()
    average(0)
    update(3)
    average(1)
    average(2)

    for number, (h, d, p, way) in enumerate(sent):
        ag_copy(h, d, p, way, number).wait_send()
    for h in range(CHUNKS):
        w_copy(h).wait_send()
    gain_copy.wait_send()

    def drain_x(k, carry):
        x_copy(k).wait_send()
        return carry

    lax.fori_loop(1, RING, drain_x, 0)

    def add_part(j, inner):
        for c in range(COLS):
            prod = ret[c, feat_rows(j), :].astype(F32) * xt[c, feat_rows(j), :].astype(F32)
            inner = inner + jnp.sum(prod.reshape(feat // 8, 8, rows), axis=0)
        return inner

    own_r.wait()
    inner = add_part(z, jnp.zeros((8, rows), F32))

    def add_return(k, inner):
        j = (z + k) % RING
        remote(dxt.at[0], ret.at[:, feat_rows(j), :], r_send.at[0], r_recv.at[j], across).wait_recv()
        return add_part(j, inner)

    average(3)
    inner = lax.fori_loop(1, RING, add_return, inner)
    mean = jnp.sum(inner, axis=0, keepdims=True) / width

    out_x = []
    for c in range(COLS):

        def finish(k, carry):
            at = pl.ds(pl.multiple_of(k * 128, 128), 128)
            part = ret[c, at, :].astype(F32) - xt[c, at, :].astype(F32) * mean
            xin[:, pl.ds(pl.multiple_of((c * side + k) * 128, 128), 128)] = (part.T * rstd).astype(BF16)
            return carry

        lax.fori_loop(0, side, finish, 0, unroll=2)
        half = pl.ds(c * side * 128, side * 128)
        copy = pltpu.make_async_copy(xin.at[:, half], ig_hbm.at[:, half], local_sem.at[2 * CHUNKS - 1 - c])
        copy.start()
        out_x.append(copy)
    new_gain_copy.wait_recv()
    gout_ref[...] = (new_gain + ng[1, 0:1, 0:feat]) * 0.5

    for h in range(CHUNKS):
        for p in range(PARTS):
            p_copy(h, p).wait_send()
            g_copy(h, p).wait_send()
    for copy in (sum_copy, new_gain_copy):
        copy.wait_send()

    def drain_r(k, carry):
        r_copy((z + k) % RING).wait_send()
        return carry

    lax.fori_loop(1, RING, drain_r, 0)
    for copy in out_x + out_w:
        copy.wait()


def run(offset, call_id, inputs, cotangent, weight, gain):
    rows, width = inputs.shape
    feat, proj = weight.shape
    sizes = chunk_sizes(proj)
    any_space = pl.BlockSpec(memory_space=pl.ANY)
    vmem = pl.BlockSpec(memory_space=pltpu.VMEM)
    dma = pltpu.SemaphoreType.DMA

    def chunks(shape, dtype):
        return [pltpu.VMEM((*shape, n), dtype) for n in sizes]

    side = (COLS, width // COLS, rows)
    return pl.pallas_call(
        partial(body, offset),
        out_shape=(
            jax.ShapeDtypeStruct((rows, width), BF16),
            jax.ShapeDtypeStruct((feat, proj), BF16),
            jax.ShapeDtypeStruct((1, feat), F32),
        ),
        in_specs=[any_space, any_space, any_space, vmem],
        out_specs=(any_space, any_space, vmem),
        scratch_shapes=[
            chunks((RING, rows), BF16),
            chunks((COLS, feat), BF16),
            chunks((COLS, feat), F32),
            chunks((feat,), BF16),
            chunks((feat,), BF16),
            chunks((feat,), BF16),
            chunks((feat,), BF16),
            pltpu.VMEM((rows, width), BF16),
            pltpu.VMEM(side, BF16),
            pltpu.VMEM((RING, COLS, feat, rows), BF16),
            pltpu.VMEM((RING, COLS, feat, rows), BF16),
            pltpu.VMEM((RING, COLS, feat, rows), F32),
            pltpu.VMEM((COLS, feat, rows), F32),
            pltpu.VMEM((COLS, feat, 128), F32),
            pltpu.VMEM((RING, COLS, feat, rows), BF16),
            pltpu.VMEM(side, BF16),
            pltpu.VMEM((COLS, 8, 512), F32),
            pltpu.VMEM((2, 8, 512), F32),
            pltpu.VMEM((2, 8, 512), F32),
            dma((2 * CHUNKS + 1 + CHUNKS * PARTS,)),
            dma((14 * CHUNKS,)),
            dma((2 * RING * CHUNKS,)),
            dma((CHUNKS,)),
            dma((CHUNKS,)),
            dma((RING,)),
            dma((RING,)),
            dma((CHUNKS * PARTS,)),
            dma((CHUNKS * PARTS,)),
            dma((RING,)),
            dma((RING,)),
            dma((CHUNKS * PARTS,)),
            dma((CHUNKS * PARTS,)),
            dma((3,)),
            dma((3,)),
        ],
        compiler_params=pltpu.CompilerParams(
            collective_id=call_id, has_side_effects=True, vmem_limit_bytes=58 * 1024 * 1024
        ),
    )(inputs, cotangent, weight, gain)


def per_device(inputs, cotangent, weight, gain, step):
    levels = lax.axis_size("rep").bit_length() - 1
    exponent = jnp.remainder(step[0], levels)
    branches = [partial(run, 1 << level, 1 + level) for level in range(levels)]
    input_gradient, weight_out, gain_out = lax.switch(
        exponent, branches, inputs, cotangent, weight[0], gain
    )
    return (input_gradient, weight_out[None], gain_out.astype(BF16))


def solution(mesh):
    in_specs = (
        P(("rep", "fsdp"), None),
        P(("rep", "fsdp"), None),
        P("rep", "fsdp", None),
        P("rep", "fsdp"),
        P(),
    )
    out_specs = (P(("rep", "fsdp"), None), P("rep", "fsdp", None), P("rep", "fsdp"))
    return jax.shard_map(
        per_device, mesh=mesh, in_specs=in_specs, out_specs=out_specs, check_vma=False
    )
```

```python
from functools import partial

import jax
import jax.numpy as jnp
from jax import lax
from jax.experimental import pallas as pl
from jax.experimental.pallas import tpu as pltpu
from jax.sharding import PartitionSpec as P

MESH = pl.DeviceIdType.MESH
F32 = jnp.float32
BF16 = jnp.bfloat16

epsilon = 1e-05
learn_rate = 0.5
gain_rate = 0.01

COLS = 2
RING = 8
CHUNKS = 4
PARTS = 2
PAIRS = RING // 2


def tiles(width, step):
    return [(at, min(step, width - at)) for at in range(0, width, step)]


def column_of(row):
    n = row.shape[1]
    i = lax.broadcasted_iota(jnp.int32, (n, n), 0)
    j = lax.broadcasted_iota(jnp.int32, (n, n), 1)
    return jnp.sum(jnp.where(i == j, row, 0.0), axis=1, keepdims=True)


def row_of(column):
    n = column.shape[0]
    i = lax.broadcasted_iota(jnp.int32, (n, n), 0)
    j = lax.broadcasted_iota(jnp.int32, (n, n), 1)
    return jnp.sum(jnp.where(i == j, column, 0.0), axis=0, keepdims=True)


def chunk_sizes(width):
    blocks = width // 128
    return [128 * (blocks // CHUNKS + (h < blocks % CHUNKS)) for h in range(CHUNKS)]


def body(
    offset,
    x_hbm, cot_hbm, w_hbm, gain_ref,
    ig_hbm, wout_hbm, gout_ref,
    cot, w, acc, pw, gp, nw, got,
    xin, xt, xc, xn, fg, gg, gb, dxt, ret, gbuf, gsum, ng,
    local_sem, ag_send, ag_recv, w_send, w_recv, x_send, x_recv, p_send, p_recv,
    r_send, r_recv, g_send, g_recv, s_send, s_recv,
):
    rows, width = xin.shape
    feat = xc.shape[2]
    sizes = [c.shape[2] for c in cot]
    starts = [sum(sizes[:h]) for h in range(CHUNKS)]
    factor = width ** (-0.5)
    part_rows = feat // PARTS

    reps = lax.axis_size("rep")
    rep = lax.axis_index("rep")
    me = lax.axis_index("fsdp")
    col = me // RING
    z = me % RING
    across = (rep, (1 - col) * RING + z)
    to_rep = (rep + offset) % reps
    from_rep = (rep + reps - offset) % reps

    def remote(src, dst, send_sem, recv_sem, device):
        return pltpu.make_async_remote_copy(
            src_ref=src, dst_ref=dst, send_sem=send_sem, recv_sem=recv_sem,
            device_id=device, device_id_type=MESH,
        )

    barrier = pltpu.get_barrier_semaphore()
    for k in range(1, RING):
        pl.semaphore_signal(
            barrier, inc=1, device_id=(rep, col * RING + (z + k) % RING), device_id_type=MESH
        )
    for device in (across, (to_rep, me), (from_rep, me)):
        pl.semaphore_signal(barrier, inc=1, device_id=device, device_id_type=MESH)

    in_cot = [
        pltpu.make_async_copy(cot_hbm.at[:, pl.ds(starts[h], sizes[h])], cot[h].at[z], local_sem.at[h])
        for h in range(CHUNKS)
    ]
    in_w = [
        pltpu.make_async_copy(
            w_hbm.at[:, pl.ds(starts[h], sizes[h])], w[h].at[col], local_sem.at[CHUNKS + h]
        )
        for h in range(CHUNKS)
    ]
    in_x = pltpu.make_async_copy(x_hbm, xin, local_sem.at[2 * CHUNKS])
    in_cot[0].start()
    in_x.start()
    for h in range(CHUNKS):
        in_w[h].start()
    for h in range(1, CHUNKS):
        in_cot[h].start()
    gbuf[col] = jnp.zeros(gbuf.shape[1:], F32)
    gbuf[col, 0:1, 0:feat] = gain_ref[...].astype(F32)

    pl.semaphore_wait(barrier, RING + 2)

    def sign(p):
        return 1 - 2 * p

    def origin(p, d):
        return (z + 2 * RING - sign(p) * d) % RING

    def half_block(h, d, p):
        return cot[h].at[origin(p, d), pl.ds(p * (rows // 2), rows // 2), :]

    def recv_of(h, d, p):
        return ag_recv.at[(h * 2 + p) * RING + origin(p, d)]

    def ag_copy(h, d, p, way, number):
        step = sign(p) if way == "lead" else -sign(p)
        return remote(
            half_block(h, d, p), half_block(h, d, p), ag_send.at[number], recv_of(h, d, p),
            (rep, col * RING + (z + RING + step) % RING),
        )

    sent = []

    def send(h, d, p, way):
        sent.append((h, d, p, way))
        ag_copy(h, d, p, way, len(sent) - 1).start()

    def arrived(h, d, p):
        remote(
            half_block(h, d, p), half_block(h, d, p), ag_send.at[0], recv_of(h, d, p), across
        ).wait_recv()

    def ring_start(h):
        in_cot[h].wait()
        for way in ("lead", "trail"):
            for p in range(2):
                send(h, 0, p, way)

    def ring_step(h, k):
        for p in range(2):
            arrived(h, k, p)
            if k <= 3:
                send(h, k, p, "lead")
        if k <= 3:
            for p in range(2):
                arrived(h, -k, p)
                if k <= 2:
                    send(h, -k, p, "trail")

    ring_start(0)

    in_x.wait()
    lanes = 512 if width % 512 == 0 else 128

    def square(k, total):
        part = xin[:, pl.ds(pl.multiple_of(k * lanes, lanes), lanes)].astype(F32)
        part = part * part
        for at, size in tiles(lanes, 128):
            total = total + part[:, at : at + size]
        return total

    total = lax.fori_loop(0, width // lanes, square, jnp.zeros((rows, 128), F32))
    rstd = lax.rsqrt(jnp.sum(total, axis=1, keepdims=True) / width + epsilon)
    side = width // COLS // 128

    def normalize(k, carry):
        for c in range(COLS):
            at = pl.multiple_of((c * side + k) * 128, 128)
            part = (xin[:, pl.ds(at, 128)].astype(F32) * rstd).astype(BF16).astype(F32)
            xt[c, pl.ds(pl.multiple_of(k * 128, 128), 128), :] = part.T.astype(BF16)
        return carry

    lax.fori_loop(0, side, normalize, 0)

    def feat_rows(j):
        return pl.ds(pl.multiple_of(j * feat, 16), feat)

    def x_copy(k):
        j = (z + k) % RING
        return remote(
            xt.at[:, feat_rows(j), :], xc.at[z], x_send.at[k], x_recv.at[z], (rep, col * RING + j)
        )

    def x_arrived(j):
        remote(xc.at[j], xc.at[j], x_send.at[0], x_recv.at[j], across).wait_recv()

    def start_x(k, carry):
        x_copy(k).start()
        return carry

    lax.fori_loop(1, RING, start_x, 0)
    own_x = pltpu.make_async_copy(xt.at[:, feat_rows(z), :], xc.at[z], local_sem.at[2 * CHUNKS])
    own_x.start()

    gain_copy = remote(gbuf.at[col], gbuf.at[col], s_send.at[0], s_recv.at[0], across)
    gain_copy.start()

    def w_copy(h):
        return remote(w[h].at[col], w[h].at[col], w_send.at[h], w_recv.at[h], across)

    for h in range(CHUNKS):
        in_w[h].wait()
        w_copy(h).start()

    gg[...] = jnp.zeros_like(gg)
    own_x.wait()

    def rows_of(p):
        return pl.ds(p * part_rows, part_rows)

    def p_copy(h, p):
        number = h * PARTS + p
        return remote(
            pw[h].at[rows_of(p), :], gp[h].at[rows_of(p), :], p_send.at[number], p_recv.at[number], across
        )

    def g_copy(h, p):
        number = h * PARTS + p
        return remote(
            nw[h].at[rows_of(p), :], got[h].at[rows_of(p), :], g_send.at[number], g_recv.at[number],
            (to_rep, me),
        )

    def by_rows(p, work):
        def some(k, carry):
            work(pl.ds(pl.multiple_of(p * part_rows + k * 16, 16), 16))
            return carry

        lax.fori_loop(0, part_rows // 16, some, 0)

    def hand_over(h):
        for p in range(PARTS):

            def work(at):
                pw[h][at, :] = acc[h][1 - col, at, :].astype(BF16)

            by_rows(p, work)
            p_copy(h, p).start()

    def update(h):
        for p in range(PARTS):
            p_copy(h, p).wait_recv()

            def work(at):
                whole = acc[h][col, at, :] + gp[h][at, :].astype(F32)
                old = w[h][col, at, :].astype(F32)
                nw[h][at, :] = (old - learn_rate * (factor * whole)).astype(BF16)

            by_rows(p, work)
            g_copy(h, p).start()

    out_w = []

    def average(h):
        for p in range(PARTS):
            g_copy(h, p).wait_recv()

            def work(at):
                both = nw[h][at, :].astype(F32) + got[h][at, :].astype(F32)
                gp[h][at, :] = (both * 0.5).astype(BF16)

            by_rows(p, work)
            copy = pltpu.make_async_copy(
                gp[h].at[rows_of(p), :],
                wout_hbm.at[rows_of(p), pl.ds(starts[h], sizes[h])],
                local_sem.at[2 * CHUNKS + 1 + h * PARTS + p],
            )
            copy.start()
            out_w.append(copy)

    def r_copy(j):
        return remote(
            dxt.at[j], ret.at[:, feat_rows(z), :], r_send.at[j], r_recv.at[z], (rep, col * RING + j)
        )

    own_r = pltpu.make_async_copy(dxt.at[z], ret.at[:, feat_rows(z), :], local_sem.at[2 * CHUNKS])

    def pair_of(t):
        return (z + RING - (t + 1)) % RING, (z + (t + 1) % PAIRS) % RING

    def weight_step(h, events, t, carry):
        for at, event in events:
            pl.when(t == at)(event)
        a, b = pair_of(t)
        if h == 0:
            x_arrived(a)

            @pl.when(t < PAIRS - 1)
            def _():
                x_arrived(b)

        @pl.when(t == 0)
        def _():
            def clear(k, carry):
                acc[h][:, pl.ds(pl.multiple_of(k * 16, 16), 16), :] = jnp.zeros((COLS, 16, sizes[h]), F32)
                return carry

            lax.fori_loop(0, feat // 16, clear, 0)

        def side_sum(c, carry):
            if h == 0:
                for j in (a, b):
                    xn[j, c] = (xc[j, c].astype(F32) * gb[c]).astype(BF16)
            lhs = jnp.concatenate([xn[a, c], xn[b, c]], axis=1)
            for at, n in tiles(sizes[h], 256):
                ct = jnp.concatenate([cot[h][a, :, pl.ds(at, n)], cot[h][b, :, pl.ds(at, n)]], axis=0)
                acc[h][c, :, pl.ds(at, n)] += jnp.dot(lhs, ct, preferred_element_type=F32)
            return carry

        return lax.fori_loop(0, COLS, side_sum, carry)

    def feature_step(h, t, carry):
        a, b = pair_of(t)
        ct = jnp.concatenate([cot[h][a], cot[h][b]], axis=0)
        def side_feature(c, carry):
            feature = lax.dot_general(
                w[h][c], ct, (((1,), (1,)), ((), ())), preferred_element_type=F32
            )
            if h == 0:
                fg[a, c] = feature[:, :rows]
                fg[b, c] = feature[:, rows:]
            elif h < CHUNKS - 1:
                fg[a, c] += feature[:, :rows]
                fg[b, c] += feature[:, rows:]
            else:
                for j, part in ((a, feature[:, :rows]), (b, feature[:, rows:])):
                    whole = factor * (fg[j, c] + part)
                    gg[c] += whole * xc[j, c].astype(F32)
                    dxt[j, c] = (whole * gb[c]).astype(BF16)
            return carry

        lax.fori_loop(0, COLS, side_feature, 0)
        if h == CHUNKS - 1:
            r_copy(a).start()

            @pl.when(t < PAIRS - 1)
            def _():
                r_copy(b).start()

        return carry

    def weight_sums(h, *events):
        lax.fori_loop(0, PAIRS, partial(weight_step, h, events), 0)

    def features(h):
        w_copy(h).wait_recv()
        lax.fori_loop(0, PAIRS, partial(feature_step, h), 0)

    ring_step(0, 1)
    ring_step(0, 2)
    ring_step(0, 3)
    ring_start(1)
    ring_step(0, 4)
    gain_copy.wait_recv()

    def spread(c, carry):
        gb[c] = jnp.broadcast_to(column_of(gbuf[c, 0:1, 0:feat]), gb.shape[1:])
        return carry

    lax.fori_loop(0, COLS, spread, 0)

    def turn_2():
        ring_start(2)
        ring_step(1, 2)

    weight_sums(0, (1, lambda: ring_step(1, 1)), (3, turn_2))
    hand_over(0)
    ring_step(1, 3)
    ring_start(3)
    ring_step(2, 1)
    ring_step(1, 4)
    weight_sums(1, (2, lambda: ring_step(2, 2)))
    hand_over(1)
    ring_step(3, 1)
    update(0)
    ring_step(2, 3)
    features(0)
    ring_step(3, 2)
    ring_step(2, 4)
    weight_sums(2)
    hand_over(2)
    ring_step(3, 3)
    update(1)
    features(1)
    features(2)
    w_copy(3).wait_recv()

    def last_step(t, carry):
        weight_step(3, (), t, 0)
        feature_step(3, t, 0)
        return carry

    lax.fori_loop(0, PAIRS - 1, last_step, 0)
    ring_step(3, 4)
    feature_step(3, jnp.int32(PAIRS - 1), 0)
    own_r.start()
    weight_step(3, (), jnp.int32(PAIRS - 1), 0)
    hand_over(3)
    update(2)

    def gain_sum(k, carry):
        side_of = (1 - col) * (1 - k) + col * k
        gsum[2 * k] = jnp.zeros(gsum.shape[1:], F32)
        gsum[2 * k, 0:1, 0:feat] = row_of(jnp.sum(gg[side_of], axis=1, keepdims=True))
        return carry

    lax.fori_loop(0, 2, gain_sum, 0)
    sum_copy = remote(gsum.at[0], gsum.at[1], s_send.at[1], s_recv.at[1], across)
    sum_copy.start()
    sum_copy.wait_recv()
    total_gain = gsum[2, 0:1, 0:feat] + gsum[1, 0:1, 0:feat]
    new_gain = (gbuf[col, 0:1, 0:feat] - gain_rate * total_gain).astype(BF16).astype(F32)
    ng[0] = jnp.zeros(ng.shape[1:], F32)
    ng[0, 0:1, 0:feat] = new_gain
    new_gain_copy = remote(ng.at[0], ng.at[1], s_send.at[2], s_recv.at[2], (to_rep, me))
    new_gain_copy.start()
    average(0)
    update(3)
    average(1)
    average(2)

    for number, (h, d, p, way) in enumerate(sent):
        ag_copy(h, d, p, way, number).wait_send()
    for h in range(CHUNKS):
        w_copy(h).wait_send()
    gain_copy.wait_send()

    def drain_x(k, carry):
        x_copy(k).wait_send()
        return carry

    lax.fori_loop(1, RING, drain_x, 0)

    def add_part(j, inner):
        for c in range(COLS):
            prod = ret[c, feat_rows(j), :].astype(F32) * xt[c, feat_rows(j), :].astype(F32)
            inner = inner + jnp.sum(prod.reshape(feat // 8, 8, rows), axis=0)
        return inner

    own_r.wait()
    inner = add_part(z, jnp.zeros((8, rows), F32))

    def add_return(k, inner):
        j = (z + k) % RING
        remote(dxt.at[0], ret.at[:, feat_rows(j), :], r_send.at[0], r_recv.at[j], across).wait_recv()
        return add_part(j, inner)

    average(3)
    inner = lax.fori_loop(1, RING, add_return, inner)
    mean = jnp.sum(inner, axis=0, keepdims=True) / width

    out_x = []
    for c in range(COLS):

        def finish(k, carry):
            at = pl.ds(pl.multiple_of(k * 128, 128), 128)
            part = ret[c, at, :].astype(F32) - xt[c, at, :].astype(F32) * mean
            xin[:, pl.ds(pl.multiple_of((c * side + k) * 128, 128), 128)] = (part.T * rstd).astype(BF16)
            return carry

        lax.fori_loop(0, side, finish, 0, unroll=2)
        half = pl.ds(c * side * 128, side * 128)
        copy = pltpu.make_async_copy(xin.at[:, half], ig_hbm.at[:, half], local_sem.at[2 * CHUNKS - 1 - c])
        copy.start()
        out_x.append(copy)
    new_gain_copy.wait_recv()
    gout_ref[...] = (new_gain + ng[1, 0:1, 0:feat]) * 0.5

    for h in range(CHUNKS):
        for p in range(PARTS):
            p_copy(h, p).wait_send()
            g_copy(h, p).wait_send()
    for copy in (sum_copy, new_gain_copy):
        copy.wait_send()

    def drain_r(k, carry):
        r_copy((z + k) % RING).wait_send()
        return carry

    lax.fori_loop(1, RING, drain_r, 0)
    for copy in out_x + out_w:
        copy.wait()


def run(offset, call_id, inputs, cotangent, weight, gain):
    rows, width = inputs.shape
    feat, proj = weight.shape
    sizes = chunk_sizes(proj)
    any_space = pl.BlockSpec(memory_space=pl.ANY)
    vmem = pl.BlockSpec(memory_space=pltpu.VMEM)
    dma = pltpu.SemaphoreType.DMA

    def chunks(shape, dtype):
        return [pltpu.VMEM((*shape, n), dtype) for n in sizes]

    side = (COLS, width // COLS, rows)
    return pl.pallas_call(
        partial(body, offset),
        out_shape=(
            jax.ShapeDtypeStruct((rows, width), BF16),
            jax.ShapeDtypeStruct((feat, proj), BF16),
            jax.ShapeDtypeStruct((1, feat), F32),
        ),
        in_specs=[any_space, any_space, any_space, vmem],
        out_specs=(any_space, any_space, vmem),
        scratch_shapes=[
            chunks((RING, rows), BF16),
            chunks((COLS, feat), BF16),
            chunks((COLS, feat), F32),
            chunks((feat,), BF16),
            chunks((feat,), BF16),
            chunks((feat,), BF16),
            chunks((feat,), BF16),
            pltpu.VMEM((rows, width), BF16),
            pltpu.VMEM(side, BF16),
            pltpu.VMEM((RING, COLS, feat, rows), BF16),
            pltpu.VMEM((RING, COLS, feat, rows), BF16),
            pltpu.VMEM((RING, COLS, feat, rows), F32),
            pltpu.VMEM((COLS, feat, rows), F32),
            pltpu.VMEM((COLS, feat, 128), F32),
            pltpu.VMEM((RING, COLS, feat, rows), BF16),
            pltpu.VMEM(side, BF16),
            pltpu.VMEM((COLS, 8, 512), F32),
            pltpu.VMEM((3, 8, 512), F32),
            pltpu.VMEM((2, 8, 512), F32),
            dma((2 * CHUNKS + 1 + CHUNKS * PARTS,)),
            dma((14 * CHUNKS,)),
            dma((2 * RING * CHUNKS,)),
            dma((CHUNKS,)),
            dma((CHUNKS,)),
            dma((RING,)),
            dma((RING,)),
            dma((CHUNKS * PARTS,)),
            dma((CHUNKS * PARTS,)),
            dma((RING,)),
            dma((RING,)),
            dma((CHUNKS * PARTS,)),
            dma((CHUNKS * PARTS,)),
            dma((3,)),
            dma((3,)),
        ],
        compiler_params=pltpu.CompilerParams(
            collective_id=call_id, has_side_effects=True, vmem_limit_bytes=58 * 1024 * 1024
        ),
    )(inputs, cotangent, weight, gain)


def per_device(inputs, cotangent, weight, gain, step):
    levels = lax.axis_size("rep").bit_length() - 1
    exponent = jnp.remainder(step[0], levels)
    branches = [partial(run, 1 << level, 1 + level) for level in range(levels)]
    input_gradient, weight_out, gain_out = lax.switch(
        exponent, branches, inputs, cotangent, weight[0], gain
    )
    return (input_gradient, weight_out[None], gain_out.astype(BF16))


def solution(mesh):
    in_specs = (
        P(("rep", "fsdp"), None),
        P(("rep", "fsdp"), None),
        P("rep", "fsdp", None),
        P("rep", "fsdp"),
        P(),
    )
    out_specs = (P(("rep", "fsdp"), None), P("rep", "fsdp", None), P("rep", "fsdp"))
    return jax.shard_map(
        per_device, mesh=mesh, in_specs=in_specs, out_specs=out_specs, check_vma=False
    )
```

```python
from functools import partial

import jax
import jax.numpy as jnp
from jax import lax
from jax.experimental import pallas as pl
from jax.experimental.pallas import tpu as pltpu
from jax.sharding import PartitionSpec as P

MESH = pl.DeviceIdType.MESH
F32 = jnp.float32
BF16 = jnp.bfloat16

epsilon = 1e-05
learn_rate = 0.5
gain_rate = 0.01

COLS = 2
RING = 8
CHUNKS = 4
PARTS = 2
PAIRS = RING // 2


def tiles(width, step):
    return [(at, min(step, width - at)) for at in range(0, width, step)]


def column_of(row):
    n = row.shape[1]
    i = lax.broadcasted_iota(jnp.int32, (n, n), 0)
    j = lax.broadcasted_iota(jnp.int32, (n, n), 1)
    return jnp.sum(jnp.where(i == j, row, 0.0), axis=1, keepdims=True)


def row_of(column):
    n = column.shape[0]
    i = lax.broadcasted_iota(jnp.int32, (n, n), 0)
    j = lax.broadcasted_iota(jnp.int32, (n, n), 1)
    return jnp.sum(jnp.where(i == j, column, 0.0), axis=0, keepdims=True)


def chunk_sizes(width):
    blocks = width // 128
    order = (1, 2, 0, 3)
    return [128 * (blocks // CHUNKS + (order.index(h) < blocks % CHUNKS)) for h in range(CHUNKS)]


def body(
    offset,
    x_hbm, cot_hbm, w_hbm, gain_ref,
    ig_hbm, wout_hbm, gout_ref,
    cot, w, acc, pw, gp, nw, got,
    xin, xt, xc, xn, fg, gg, gb, dxt, ret, gbuf, gsum, ng,
    local_sem, ag_send, ag_recv, w_send, w_recv, x_send, x_recv, p_send, p_recv,
    r_send, r_recv, g_send, g_recv, s_send, s_recv,
):
    rows, width = xin.shape
    feat = xc.shape[2]
    sizes = [c.shape[2] for c in cot]
    starts = [sum(sizes[:h]) for h in range(CHUNKS)]
    factor = width ** (-0.5)
    part_rows = feat // PARTS

    reps = lax.axis_size("rep")
    rep = lax.axis_index("rep")
    me = lax.axis_index("fsdp")
    col = me // RING
    z = me % RING
    across = (rep, (1 - col) * RING + z)
    to_rep = (rep + offset) % reps
    from_rep = (rep + reps - offset) % reps

    def remote(src, dst, send_sem, recv_sem, device):
        return pltpu.make_async_remote_copy(
            src_ref=src, dst_ref=dst, send_sem=send_sem, recv_sem=recv_sem,
            device_id=device, device_id_type=MESH,
        )

    barrier = pltpu.get_barrier_semaphore()
    for k in range(1, RING):
        pl.semaphore_signal(
            barrier, inc=1, device_id=(rep, col * RING + (z + k) % RING), device_id_type=MESH
        )
    for device in (across, (to_rep, me), (from_rep, me)):
        pl.semaphore_signal(barrier, inc=1, device_id=device, device_id_type=MESH)

    in_cot = [
        pltpu.make_async_copy(cot_hbm.at[:, pl.ds(starts[h], sizes[h])], cot[h].at[z], local_sem.at[h])
        for h in range(CHUNKS)
    ]
    in_w = [
        pltpu.make_async_copy(
            w_hbm.at[:, pl.ds(starts[h], sizes[h])], w[h].at[col], local_sem.at[CHUNKS + h]
        )
        for h in range(CHUNKS)
    ]
    in_x = pltpu.make_async_copy(x_hbm, xin, local_sem.at[2 * CHUNKS])
    in_cot[0].start()
    in_x.start()
    for h in range(CHUNKS):
        in_w[h].start()
    for h in range(1, CHUNKS):
        in_cot[h].start()
    gbuf[col] = jnp.zeros(gbuf.shape[1:], F32)
    gbuf[col, 0:1, 0:feat] = gain_ref[...].astype(F32)

    pl.semaphore_wait(barrier, RING + 2)

    def sign(p):
        return 1 - 2 * p

    def origin(p, d):
        return (z + 2 * RING - sign(p) * d) % RING

    def half_block(h, d, p):
        return cot[h].at[origin(p, d), pl.ds(p * (rows // 2), rows // 2), :]

    def recv_of(h, d, p):
        return ag_recv.at[(h * 2 + p) * RING + origin(p, d)]

    def ag_copy(h, d, p, way, number):
        step = sign(p) if way == "lead" else -sign(p)
        return remote(
            half_block(h, d, p), half_block(h, d, p), ag_send.at[number], recv_of(h, d, p),
            (rep, col * RING + (z + RING + step) % RING),
        )

    sent = []

    def send(h, d, p, way):
        sent.append((h, d, p, way))
        ag_copy(h, d, p, way, len(sent) - 1).start()

    def arrived(h, d, p):
        remote(
            half_block(h, d, p), half_block(h, d, p), ag_send.at[0], recv_of(h, d, p), across
        ).wait_recv()

    def ring_start(h):
        in_cot[h].wait()
        for way in ("lead", "trail"):
            for p in range(2):
                send(h, 0, p, way)

    def ring_step(h, k):
        for p in range(2):
            arrived(h, k, p)
            if k <= 3:
                send(h, k, p, "lead")
        if k <= 3:
            for p in range(2):
                arrived(h, -k, p)
                if k <= 2:
                    send(h, -k, p, "trail")

    ring_start(0)

    in_x.wait()
    lanes = 512 if width % 512 == 0 else 128

    def square(k, total):
        part = xin[:, pl.ds(pl.multiple_of(k * lanes, lanes), lanes)].astype(F32)
        part = part * part
        for at, size in tiles(lanes, 128):
            total = total + part[:, at : at + size]
        return total

    total = lax.fori_loop(0, width // lanes, square, jnp.zeros((rows, 128), F32))
    rstd = lax.rsqrt(jnp.sum(total, axis=1, keepdims=True) / width + epsilon)
    side = width // COLS // 128

    def normalize(k, carry):
        for c in range(COLS):
            at = pl.multiple_of((c * side + k) * 128, 128)
            part = (xin[:, pl.ds(at, 128)].astype(F32) * rstd).astype(BF16).astype(F32)
            xt[c, pl.ds(pl.multiple_of(k * 128, 128), 128), :] = part.T.astype(BF16)
        return carry

    lax.fori_loop(0, side, normalize, 0)

    def feat_rows(j):
        return pl.ds(pl.multiple_of(j * feat, 16), feat)

    def x_copy(k):
        j = (z + k) % RING
        return remote(
            xt.at[:, feat_rows(j), :], xc.at[z], x_send.at[k], x_recv.at[z], (rep, col * RING + j)
        )

    def x_arrived(j):
        remote(xc.at[j], xc.at[j], x_send.at[0], x_recv.at[j], across).wait_recv()

    def start_x(k, carry):
        x_copy(k).start()
        return carry

    lax.fori_loop(1, RING, start_x, 0)
    own_x = pltpu.make_async_copy(xt.at[:, feat_rows(z), :], xc.at[z], local_sem.at[2 * CHUNKS])
    own_x.start()

    gain_copy = remote(gbuf.at[col], gbuf.at[col], s_send.at[0], s_recv.at[0], across)
    gain_copy.start()

    def w_copy(h):
        return remote(w[h].at[col], w[h].at[col], w_send.at[h], w_recv.at[h], across)

    for h in range(CHUNKS):
        in_w[h].wait()
        w_copy(h).start()

    gg[...] = jnp.zeros_like(gg)
    own_x.wait()

    def rows_of(p):
        return pl.ds(p * part_rows, part_rows)

    def p_copy(h, p):
        number = h * PARTS + p
        return remote(
            pw[h].at[rows_of(p), :], gp[h].at[rows_of(p), :], p_send.at[number], p_recv.at[number], across
        )

    def g_copy(h, p):
        number = h * PARTS + p
        return remote(
            nw[h].at[rows_of(p), :], got[h].at[rows_of(p), :], g_send.at[number], g_recv.at[number],
            (to_rep, me),
        )

    def by_rows(p, work):
        def some(k, carry):
            work(pl.ds(pl.multiple_of(p * part_rows + k * 16, 16), 16))
            return carry

        lax.fori_loop(0, part_rows // 16, some, 0)

    def hand_over(h):
        for p in range(PARTS):

            def work(at):
                pw[h][at, :] = acc[h][1 - col, at, :].astype(BF16)

            by_rows(p, work)
            p_copy(h, p).start()

    def update(h):
        for p in range(PARTS):
            p_copy(h, p).wait_recv()

            def work(at):
                whole = acc[h][col, at, :] + gp[h][at, :].astype(F32)
                old = w[h][col, at, :].astype(F32)
                nw[h][at, :] = (old - learn_rate * (factor * whole)).astype(BF16)

            by_rows(p, work)
            g_copy(h, p).start()

    out_w = []

    def average(h):
        for p in range(PARTS):
            g_copy(h, p).wait_recv()

            def work(at):
                both = nw[h][at, :].astype(F32) + got[h][at, :].astype(F32)
                gp[h][at, :] = (both * 0.5).astype(BF16)

            by_rows(p, work)
            copy = pltpu.make_async_copy(
                gp[h].at[rows_of(p), :],
                wout_hbm.at[rows_of(p), pl.ds(starts[h], sizes[h])],
                local_sem.at[2 * CHUNKS + 1 + h * PARTS + p],
            )
            copy.start()
            out_w.append(copy)

    def r_copy(j):
        return remote(
            dxt.at[j], ret.at[:, feat_rows(z), :], r_send.at[j], r_recv.at[z], (rep, col * RING + j)
        )

    own_r = pltpu.make_async_copy(dxt.at[z], ret.at[:, feat_rows(z), :], local_sem.at[2 * CHUNKS])

    def pair_of(t):
        return (z + RING - (t + 1)) % RING, (z + (t + 1) % PAIRS) % RING

    def weight_step(h, events, t, carry):
        for at, event in events:
            pl.when(t == at)(event)
        a, b = pair_of(t)
        if h == 0:
            x_arrived(a)

            @pl.when(t < PAIRS - 1)
            def _():
                x_arrived(b)

        @pl.when(t == 0)
        def _():
            def clear(k, carry):
                acc[h][:, pl.ds(pl.multiple_of(k * 16, 16), 16), :] = jnp.zeros((COLS, 16, sizes[h]), F32)
                return carry

            lax.fori_loop(0, feat // 16, clear, 0)

        def side_sum(c, carry):
            if h == 0:
                for j in (a, b):
                    xn[j, c] = (xc[j, c].astype(F32) * gb[c]).astype(BF16)
            lhs = jnp.concatenate([xn[a, c], xn[b, c]], axis=1)
            for at, n in tiles(sizes[h], 256):
                ct = jnp.concatenate([cot[h][a, :, pl.ds(at, n)], cot[h][b, :, pl.ds(at, n)]], axis=0)
                acc[h][c, :, pl.ds(at, n)] += jnp.dot(lhs, ct, preferred_element_type=F32)
            return carry

        return lax.fori_loop(0, COLS, side_sum, carry)

    def feature_step(h, t, carry):
        a, b = pair_of(t)
        ct = jnp.concatenate([cot[h][a], cot[h][b]], axis=0)
        def side_feature(c, carry):
            feature = lax.dot_general(
                w[h][c], ct, (((1,), (1,)), ((), ())), preferred_element_type=F32
            )
            if h == 0:
                fg[a, c] = feature[:, :rows]
                fg[b, c] = feature[:, rows:]
            elif h < CHUNKS - 1:
                fg[a, c] += feature[:, :rows]
                fg[b, c] += feature[:, rows:]
            else:
                for j, part in ((a, feature[:, :rows]), (b, feature[:, rows:])):
                    whole = factor * (fg[j, c] + part)
                    gg[c] += whole * xc[j, c].astype(F32)
                    dxt[j, c] = (whole * gb[c]).astype(BF16)
            return carry

        lax.fori_loop(0, COLS, side_feature, 0)
        if h == CHUNKS - 1:
            r_copy(a).start()

            @pl.when(t < PAIRS - 1)
            def _():
                r_copy(b).start()

        return carry

    def weight_sums(h, *events):
        lax.fori_loop(0, PAIRS, partial(weight_step, h, events), 0)

    def features(h):
        w_copy(h).wait_recv()
        lax.fori_loop(0, PAIRS, partial(feature_step, h), 0)

    ring_step(0, 1)
    ring_step(0, 2)
    ring_step(0, 3)
    ring_start(1)
    ring_step(0, 4)
    gain_copy.wait_recv()

    def spread(c, carry):
        gb[c] = jnp.broadcast_to(column_of(gbuf[c, 0:1, 0:feat]), gb.shape[1:])
        return carry

    lax.fori_loop(0, COLS, spread, 0)

    def turn_2():
        ring_start(2)
        ring_step(1, 2)

    weight_sums(0, (1, lambda: ring_step(1, 1)), (3, turn_2))
    hand_over(0)
    ring_step(1, 3)
    ring_start(3)
    ring_step(2, 1)
    ring_step(1, 4)
    weight_sums(1, (2, lambda: ring_step(2, 2)))
    hand_over(1)
    ring_step(3, 1)
    update(0)
    ring_step(2, 3)
    features(0)
    ring_step(3, 2)
    ring_step(2, 4)
    weight_sums(2)
    hand_over(2)
    ring_step(3, 3)
    update(1)
    features(1)
    features(2)
    w_copy(3).wait_recv()

    def last_step(t, carry):
        weight_step(3, (), t, 0)
        feature_step(3, t, 0)
        return carry

    lax.fori_loop(0, PAIRS - 1, last_step, 0)
    ring_step(3, 4)
    feature_step(3, jnp.int32(PAIRS - 1), 0)
    own_r.start()
    weight_step(3, (), jnp.int32(PAIRS - 1), 0)
    hand_over(3)
    update(2)

    def gain_sum(k, carry):
        side_of = (1 - col) * (1 - k) + col * k
        gsum[2 * k] = jnp.zeros(gsum.shape[1:], F32)
        gsum[2 * k, 0:1, 0:feat] = row_of(jnp.sum(gg[side_of], axis=1, keepdims=True))
        return carry

    lax.fori_loop(0, 2, gain_sum, 0)
    sum_copy = remote(gsum.at[0], gsum.at[1], s_send.at[1], s_recv.at[1], across)
    sum_copy.start()
    sum_copy.wait_recv()
    total_gain = gsum[2, 0:1, 0:feat] + gsum[1, 0:1, 0:feat]
    new_gain = (gbuf[col, 0:1, 0:feat] - gain_rate * total_gain).astype(BF16).astype(F32)
    ng[0] = jnp.zeros(ng.shape[1:], F32)
    ng[0, 0:1, 0:feat] = new_gain
    new_gain_copy = remote(ng.at[0], ng.at[1], s_send.at[2], s_recv.at[2], (to_rep, me))
    new_gain_copy.start()
    average(0)
    update(3)
    average(1)
    average(2)

    for number, (h, d, p, way) in enumerate(sent):
        ag_copy(h, d, p, way, number).wait_send()
    for h in range(CHUNKS):
        w_copy(h).wait_send()
    gain_copy.wait_send()

    def drain_x(k, carry):
        x_copy(k).wait_send()
        return carry

    lax.fori_loop(1, RING, drain_x, 0)

    def add_part(j, inner):
        for c in range(COLS):
            prod = ret[c, feat_rows(j), :].astype(F32) * xt[c, feat_rows(j), :].astype(F32)
            inner = inner + jnp.sum(prod.reshape(feat // 8, 8, rows), axis=0)
        return inner

    own_r.wait()
    inner = add_part(z, jnp.zeros((8, rows), F32))

    def add_return(k, inner):
        j = (z + k) % RING
        remote(dxt.at[0], ret.at[:, feat_rows(j), :], r_send.at[0], r_recv.at[j], across).wait_recv()
        return add_part(j, inner)

    average(3)
    inner = lax.fori_loop(1, RING, add_return, inner)
    mean = jnp.sum(inner, axis=0, keepdims=True) / width

    out_x = []
    for c in range(COLS):

        def finish(k, carry):
            at = pl.ds(pl.multiple_of(k * 128, 128), 128)
            part = ret[c, at, :].astype(F32) - xt[c, at, :].astype(F32) * mean
            xin[:, pl.ds(pl.multiple_of((c * side + k) * 128, 128), 128)] = (part.T * rstd).astype(BF16)
            return carry

        lax.fori_loop(0, side, finish, 0, unroll=2)
        half = pl.ds(c * side * 128, side * 128)
        copy = pltpu.make_async_copy(xin.at[:, half], ig_hbm.at[:, half], local_sem.at[2 * CHUNKS - 1 - c])
        copy.start()
        out_x.append(copy)
    new_gain_copy.wait_recv()
    gout_ref[...] = (new_gain + ng[1, 0:1, 0:feat]) * 0.5

    for h in range(CHUNKS):
        for p in range(PARTS):
            p_copy(h, p).wait_send()
            g_copy(h, p).wait_send()
    for copy in (sum_copy, new_gain_copy):
        copy.wait_send()

    def drain_r(k, carry):
        r_copy((z + k) % RING).wait_send()
        return carry

    lax.fori_loop(1, RING, drain_r, 0)
    for copy in out_x + out_w:
        copy.wait()


def run(offset, call_id, inputs, cotangent, weight, gain):
    rows, width = inputs.shape
    feat, proj = weight.shape
    sizes = chunk_sizes(proj)
    any_space = pl.BlockSpec(memory_space=pl.ANY)
    vmem = pl.BlockSpec(memory_space=pltpu.VMEM)
    dma = pltpu.SemaphoreType.DMA

    def chunks(shape, dtype):
        return [pltpu.VMEM((*shape, n), dtype) for n in sizes]

    side = (COLS, width // COLS, rows)
    return pl.pallas_call(
        partial(body, offset),
        out_shape=(
            jax.ShapeDtypeStruct((rows, width), BF16),
            jax.ShapeDtypeStruct((feat, proj), BF16),
            jax.ShapeDtypeStruct((1, feat), F32),
        ),
        in_specs=[any_space, any_space, any_space, vmem],
        out_specs=(any_space, any_space, vmem),
        scratch_shapes=[
            chunks((RING, rows), BF16),
            chunks((COLS, feat), BF16),
            chunks((COLS, feat), F32),
            chunks((feat,), BF16),
            chunks((feat,), BF16),
            chunks((feat,), BF16),
            chunks((feat,), BF16),
            pltpu.VMEM((rows, width), BF16),
            pltpu.VMEM(side, BF16),
            pltpu.VMEM((RING, COLS, feat, rows), BF16),
            pltpu.VMEM((RING, COLS, feat, rows), BF16),
            pltpu.VMEM((RING, COLS, feat, rows), F32),
            pltpu.VMEM((COLS, feat, rows), F32),
            pltpu.VMEM((COLS, feat, 128), F32),
            pltpu.VMEM((RING, COLS, feat, rows), BF16),
            pltpu.VMEM(side, BF16),
            pltpu.VMEM((COLS, 8, 512), F32),
            pltpu.VMEM((3, 8, 512), F32),
            pltpu.VMEM((2, 8, 512), F32),
            dma((2 * CHUNKS + 1 + CHUNKS * PARTS,)),
            dma((14 * CHUNKS,)),
            dma((2 * RING * CHUNKS,)),
            dma((CHUNKS,)),
            dma((CHUNKS,)),
            dma((RING,)),
            dma((RING,)),
            dma((CHUNKS * PARTS,)),
            dma((CHUNKS * PARTS,)),
            dma((RING,)),
            dma((RING,)),
            dma((CHUNKS * PARTS,)),
            dma((CHUNKS * PARTS,)),
            dma((3,)),
            dma((3,)),
        ],
        compiler_params=pltpu.CompilerParams(
            collective_id=call_id, has_side_effects=True, vmem_limit_bytes=58 * 1024 * 1024
        ),
    )(inputs, cotangent, weight, gain)


def per_device(inputs, cotangent, weight, gain, step):
    levels = lax.axis_size("rep").bit_length() - 1
    exponent = jnp.remainder(step[0], levels)
    branches = [partial(run, 1 << level, 1 + level) for level in range(levels)]
    input_gradient, weight_out, gain_out = lax.switch(
        exponent, branches, inputs, cotangent, weight[0], gain
    )
    return (input_gradient, weight_out[None], gain_out.astype(BF16))


def solution(mesh):
    in_specs = (
        P(("rep", "fsdp"), None),
        P(("rep", "fsdp"), None),
        P("rep", "fsdp", None),
        P("rep", "fsdp"),
        P(),
    )
    out_specs = (P(("rep", "fsdp"), None), P("rep", "fsdp", None), P("rep", "fsdp"))
    return jax.shard_map(
        per_device, mesh=mesh, in_specs=in_specs, out_specs=out_specs, check_vma=False
    )
```

```python
from functools import partial

import jax
import jax.numpy as jnp
from jax import lax
from jax.experimental import pallas as pl
from jax.experimental.pallas import tpu as pltpu
from jax.sharding import PartitionSpec as P

MESH = pl.DeviceIdType.MESH
F32 = jnp.float32
BF16 = jnp.bfloat16

epsilon = 1e-05
learn_rate = 0.5
gain_rate = 0.01

COLS = 2
RING = 8
CHUNKS = 4
PARTS = 2
PAIRS = RING // 2


def tiles(width, step):
    return [(at, min(step, width - at)) for at in range(0, width, step)]


def column_of(row):
    n = row.shape[1]
    i = lax.broadcasted_iota(jnp.int32, (n, n), 0)
    j = lax.broadcasted_iota(jnp.int32, (n, n), 1)
    return jnp.sum(jnp.where(i == j, row, 0.0), axis=1, keepdims=True)


def row_of(column):
    n = column.shape[0]
    i = lax.broadcasted_iota(jnp.int32, (n, n), 0)
    j = lax.broadcasted_iota(jnp.int32, (n, n), 1)
    return jnp.sum(jnp.where(i == j, column, 0.0), axis=0, keepdims=True)


def chunk_sizes(width):
    blocks = width // 128
    order = (1, 2, 0, 3)
    return [128 * (blocks // CHUNKS + (order.index(h) < blocks % CHUNKS)) for h in range(CHUNKS)]


def body(
    offset,
    x_hbm, cot_hbm, w_hbm, gain_ref,
    ig_hbm, wout_hbm, gout_ref,
    cot, w, acc, pw, gp, nw, got,
    xin, xt, xc, xn, fg, gg, gb, dxt, ret, gbuf, gsum, ng,
    local_sem, ag_send, ag_recv, w_send, w_recv, x_send, x_recv, p_send, p_recv,
    r_send, r_recv, g_send, g_recv, s_send, s_recv,
):
    rows, width = xin.shape
    feat = xc.shape[2]
    sizes = [c.shape[2] for c in cot]
    starts = [sum(sizes[:h]) for h in range(CHUNKS)]
    factor = width ** (-0.5)
    part_rows = feat // PARTS

    reps = lax.axis_size("rep")
    rep = lax.axis_index("rep")
    me = lax.axis_index("fsdp")
    col = me // RING
    z = me % RING
    across = (rep, (1 - col) * RING + z)
    to_rep = (rep + offset) % reps
    from_rep = (rep + reps - offset) % reps

    def remote(src, dst, send_sem, recv_sem, device):
        return pltpu.make_async_remote_copy(
            src_ref=src, dst_ref=dst, send_sem=send_sem, recv_sem=recv_sem,
            device_id=device, device_id_type=MESH,
        )

    barrier = pltpu.get_barrier_semaphore()
    for k in range(1, RING):
        pl.semaphore_signal(
            barrier, inc=1, device_id=(rep, col * RING + (z + k) % RING), device_id_type=MESH
        )
    for device in (across, (to_rep, me), (from_rep, me)):
        pl.semaphore_signal(barrier, inc=1, device_id=device, device_id_type=MESH)

    in_cot = [
        pltpu.make_async_copy(cot_hbm.at[:, pl.ds(starts[h], sizes[h])], cot[h].at[z], local_sem.at[h])
        for h in range(CHUNKS)
    ]
    in_w = [
        pltpu.make_async_copy(
            w_hbm.at[:, pl.ds(starts[h], sizes[h])], w[h].at[col], local_sem.at[CHUNKS + h]
        )
        for h in range(CHUNKS)
    ]
    in_x = pltpu.make_async_copy(x_hbm, xin, local_sem.at[2 * CHUNKS])
    in_cot[0].start()
    in_x.start()
    for h in range(CHUNKS):
        in_w[h].start()
    for h in range(1, CHUNKS):
        in_cot[h].start()
    gbuf[col] = jnp.zeros(gbuf.shape[1:], F32)
    gbuf[col, 0:1, 0:feat] = gain_ref[...].astype(F32)

    pl.semaphore_wait(barrier, RING + 2)

    def sign(p):
        return 1 - 2 * p

    def origin(p, d):
        return (z + 2 * RING - sign(p) * d) % RING

    def half_block(h, d, p):
        return cot[h].at[origin(p, d), pl.ds(p * (rows // 2), rows // 2), :]

    def recv_of(h, d, p):
        return ag_recv.at[(h * 2 + p) * RING + origin(p, d)]

    def ag_copy(h, d, p, way, number):
        step = sign(p) if way == "lead" else -sign(p)
        return remote(
            half_block(h, d, p), half_block(h, d, p), ag_send.at[number], recv_of(h, d, p),
            (rep, col * RING + (z + RING + step) % RING),
        )

    sent = []

    def send(h, d, p, way):
        sent.append((h, d, p, way))
        ag_copy(h, d, p, way, len(sent) - 1).start()

    def arrived(h, d, p):
        remote(
            half_block(h, d, p), half_block(h, d, p), ag_send.at[0], recv_of(h, d, p), across
        ).wait_recv()

    def ring_start(h):
        in_cot[h].wait()
        for way in ("lead", "trail"):
            for p in range(2):
                send(h, 0, p, way)

    def ring_step(h, k):
        for p in range(2):
            arrived(h, k, p)
            if k <= 3:
                send(h, k, p, "lead")
        if k <= 3:
            for p in range(2):
                arrived(h, -k, p)
                if k <= 2:
                    send(h, -k, p, "trail")

    ring_start(0)

    gain_copy = remote(gbuf.at[col], gbuf.at[col], s_send.at[0], s_recv.at[0], across)
    gain_copy.start()

    def w_copy(h):
        return remote(w[h].at[col], w[h].at[col], w_send.at[h], w_recv.at[h], across)

    for h in range(CHUNKS):
        in_w[h].wait()
        w_copy(h).start()

    in_x.wait()
    lanes = 512 if width % 512 == 0 else 128

    def square(k, total):
        part = xin[:, pl.ds(pl.multiple_of(k * lanes, lanes), lanes)].astype(F32)
        part = part * part
        for at, size in tiles(lanes, 128):
            total = total + part[:, at : at + size]
        return total

    total = lax.fori_loop(0, width // lanes, square, jnp.zeros((rows, 128), F32))
    rstd = lax.rsqrt(jnp.sum(total, axis=1, keepdims=True) / width + epsilon)
    side = width // COLS // 128

    def normalize(k, carry):
        for c in range(COLS):
            at = pl.multiple_of((c * side + k) * 128, 128)
            part = (xin[:, pl.ds(at, 128)].astype(F32) * rstd).astype(BF16).astype(F32)
            xt[c, pl.ds(pl.multiple_of(k * 128, 128), 128), :] = part.T.astype(BF16)
        return carry

    lax.fori_loop(0, side, normalize, 0)

    def feat_rows(j):
        return pl.ds(pl.multiple_of(j * feat, 16), feat)

    def x_copy(k):
        j = (z + k) % RING
        return remote(
            xt.at[:, feat_rows(j), :], xc.at[z], x_send.at[k], x_recv.at[z], (rep, col * RING + j)
        )

    def x_arrived(j):
        remote(xc.at[j], xc.at[j], x_send.at[0], x_recv.at[j], across).wait_recv()

    def start_x(k, carry):
        x_copy(k).start()
        return carry

    lax.fori_loop(1, RING, start_x, 0)
    own_x = pltpu.make_async_copy(xt.at[:, feat_rows(z), :], xc.at[z], local_sem.at[2 * CHUNKS])
    own_x.start()

    gg[...] = jnp.zeros_like(gg)
    own_x.wait()

    def rows_of(p):
        return pl.ds(p * part_rows, part_rows)

    def p_copy(h, p):
        number = h * PARTS + p
        return remote(
            pw[h].at[rows_of(p), :], gp[h].at[rows_of(p), :], p_send.at[number], p_recv.at[number], across
        )

    def g_copy(h, p):
        number = h * PARTS + p
        return remote(
            nw[h].at[rows_of(p), :], got[h].at[rows_of(p), :], g_send.at[number], g_recv.at[number],
            (to_rep, me),
        )

    def by_rows(p, work):
        def some(k, carry):
            work(pl.ds(pl.multiple_of(p * part_rows + k * 16, 16), 16))
            return carry

        lax.fori_loop(0, part_rows // 16, some, 0)

    def hand_over(h):
        for p in range(PARTS):

            def work(at):
                pw[h][at, :] = acc[h][1 - col, at, :].astype(BF16)

            by_rows(p, work)
            p_copy(h, p).start()

    def update(h):
        for p in range(PARTS):
            p_copy(h, p).wait_recv()

            def work(at):
                whole = acc[h][col, at, :] + gp[h][at, :].astype(F32)
                old = w[h][col, at, :].astype(F32)
                nw[h][at, :] = (old - learn_rate * (factor * whole)).astype(BF16)

            by_rows(p, work)
            g_copy(h, p).start()

    out_w = []

    def average(h):
        for p in range(PARTS):
            g_copy(h, p).wait_recv()

            def work(at):
                both = nw[h][at, :].astype(F32) + got[h][at, :].astype(F32)
                gp[h][at, :] = (both * 0.5).astype(BF16)

            by_rows(p, work)
            copy = pltpu.make_async_copy(
                gp[h].at[rows_of(p), :],
                wout_hbm.at[rows_of(p), pl.ds(starts[h], sizes[h])],
                local_sem.at[2 * CHUNKS + 1 + h * PARTS + p],
            )
            copy.start()
            out_w.append(copy)

    def r_copy(j):
        return remote(
            dxt.at[j], ret.at[:, feat_rows(z), :], r_send.at[j], r_recv.at[z], (rep, col * RING + j)
        )

    own_r = pltpu.make_async_copy(dxt.at[z], ret.at[:, feat_rows(z), :], local_sem.at[2 * CHUNKS])

    def pair_of(t):
        return (z + RING - (t + 1)) % RING, (z + (t + 1) % PAIRS) % RING

    def weight_step(h, events, t, carry):
        for at, event in events:
            pl.when(t == at)(event)
        a, b = pair_of(t)
        if h == 0:
            x_arrived(a)

            @pl.when(t < PAIRS - 1)
            def _():
                x_arrived(b)

        @pl.when(t == 0)
        def _():
            def clear(k, carry):
                acc[h][:, pl.ds(pl.multiple_of(k * 16, 16), 16), :] = jnp.zeros((COLS, 16, sizes[h]), F32)
                return carry

            lax.fori_loop(0, feat // 16, clear, 0)

        def side_sum(c, carry):
            if h == 0:
                for j in (a, b):
                    xn[j, c] = (xc[j, c].astype(F32) * gb[c]).astype(BF16)
            lhs = jnp.concatenate([xn[a, c], xn[b, c]], axis=1)
            for at, n in tiles(sizes[h], 256):
                ct = jnp.concatenate([cot[h][a, :, pl.ds(at, n)], cot[h][b, :, pl.ds(at, n)]], axis=0)
                acc[h][c, :, pl.ds(at, n)] += jnp.dot(lhs, ct, preferred_element_type=F32)
            return carry

        return lax.fori_loop(0, COLS, side_sum, carry)

    def feature_step(h, t, carry):
        a, b = pair_of(t)
        ct = jnp.concatenate([cot[h][a], cot[h][b]], axis=0)
        def side_feature(c, carry):
            feature = lax.dot_general(
                w[h][c], ct, (((1,), (1,)), ((), ())), preferred_element_type=F32
            )
            if h == 0:
                fg[a, c] = feature[:, :rows]
                fg[b, c] = feature[:, rows:]
            elif h < CHUNKS - 1:
                fg[a, c] += feature[:, :rows]
                fg[b, c] += feature[:, rows:]
            else:
                for j, part in ((a, feature[:, :rows]), (b, feature[:, rows:])):
                    whole = factor * (fg[j, c] + part)
                    gg[c] += whole * xc[j, c].astype(F32)
                    dxt[j, c] = (whole * gb[c]).astype(BF16)
            return carry

        lax.fori_loop(0, COLS, side_feature, 0)
        if h == CHUNKS - 1:
            r_copy(a).start()

            @pl.when(t < PAIRS - 1)
            def _():
                r_copy(b).start()

        return carry

    def weight_sums(h, *events):
        lax.fori_loop(0, PAIRS, partial(weight_step, h, events), 0)

    def features(h):
        w_copy(h).wait_recv()
        lax.fori_loop(0, PAIRS, partial(feature_step, h), 0)

    ring_step(0, 1)
    ring_step(0, 2)
    ring_step(0, 3)
    ring_start(1)
    ring_step(0, 4)
    gain_copy.wait_recv()

    def spread(c, carry):
        gb[c] = jnp.broadcast_to(column_of(gbuf[c, 0:1, 0:feat]), gb.shape[1:])
        return carry

    lax.fori_loop(0, COLS, spread, 0)

    def turn_2():
        ring_start(2)
        ring_step(1, 2)

    weight_sums(0, (1, lambda: ring_step(1, 1)), (3, turn_2))
    hand_over(0)
    ring_step(1, 3)
    ring_start(3)
    ring_step(2, 1)
    ring_step(1, 4)
    weight_sums(1, (2, lambda: ring_step(2, 2)))
    hand_over(1)
    ring_step(3, 1)
    update(0)
    ring_step(2, 3)
    features(0)
    ring_step(3, 2)
    ring_step(2, 4)
    weight_sums(2)
    hand_over(2)
    ring_step(3, 3)
    update(1)
    features(1)
    features(2)
    w_copy(3).wait_recv()

    def last_step(t, carry):
        weight_step(3, (), t, 0)
        feature_step(3, t, 0)
        return carry

    lax.fori_loop(0, PAIRS - 1, last_step, 0)
    ring_step(3, 4)
    feature_step(3, jnp.int32(PAIRS - 1), 0)
    own_r.start()
    weight_step(3, (), jnp.int32(PAIRS - 1), 0)
    hand_over(3)
    update(2)

    def gain_sum(k, carry):
        side_of = (1 - col) * (1 - k) + col * k
        gsum[2 * k] = jnp.zeros(gsum.shape[1:], F32)
        gsum[2 * k, 0:1, 0:feat] = row_of(jnp.sum(gg[side_of], axis=1, keepdims=True))
        return carry

    lax.fori_loop(0, 2, gain_sum, 0)
    sum_copy = remote(gsum.at[0], gsum.at[1], s_send.at[1], s_recv.at[1], across)
    sum_copy.start()
    sum_copy.wait_recv()
    total_gain = gsum[2, 0:1, 0:feat] + gsum[1, 0:1, 0:feat]
    new_gain = (gbuf[col, 0:1, 0:feat] - gain_rate * total_gain).astype(BF16).astype(F32)
    ng[0] = jnp.zeros(ng.shape[1:], F32)
    ng[0, 0:1, 0:feat] = new_gain
    new_gain_copy = remote(ng.at[0], ng.at[1], s_send.at[2], s_recv.at[2], (to_rep, me))
    new_gain_copy.start()
    average(0)
    update(3)
    average(1)
    average(2)

    for number, (h, d, p, way) in enumerate(sent):
        ag_copy(h, d, p, way, number).wait_send()
    for h in range(CHUNKS):
        w_copy(h).wait_send()
    gain_copy.wait_send()

    def drain_x(k, carry):
        x_copy(k).wait_send()
        return carry

    lax.fori_loop(1, RING, drain_x, 0)

    def add_part(j, inner):
        for c in range(COLS):
            prod = ret[c, feat_rows(j), :].astype(F32) * xt[c, feat_rows(j), :].astype(F32)
            inner = inner + jnp.sum(prod.reshape(feat // 8, 8, rows), axis=0)
        return inner

    own_r.wait()
    inner = add_part(z, jnp.zeros((8, rows), F32))

    def add_return(k, inner):
        j = (z + k) % RING
        remote(dxt.at[0], ret.at[:, feat_rows(j), :], r_send.at[0], r_recv.at[j], across).wait_recv()
        return add_part(j, inner)

    average(3)
    inner = lax.fori_loop(1, RING, add_return, inner)
    mean = jnp.sum(inner, axis=0, keepdims=True) / width

    out_x = []
    for c in range(COLS):

        def finish(k, carry):
            at = pl.ds(pl.multiple_of(k * 128, 128), 128)
            part = ret[c, at, :].astype(F32) - xt[c, at, :].astype(F32) * mean
            xin[:, pl.ds(pl.multiple_of((c * side + k) * 128, 128), 128)] = (part.T * rstd).astype(BF16)
            return carry

        lax.fori_loop(0, side, finish, 0, unroll=2)
        half = pl.ds(c * side * 128, side * 128)
        copy = pltpu.make_async_copy(xin.at[:, half], ig_hbm.at[:, half], local_sem.at[2 * CHUNKS - 1 - c])
        copy.start()
        out_x.append(copy)
    new_gain_copy.wait_recv()
    gout_ref[...] = (new_gain + ng[1, 0:1, 0:feat]) * 0.5

    for h in range(CHUNKS):
        for p in range(PARTS):
            p_copy(h, p).wait_send()
            g_copy(h, p).wait_send()
    for copy in (sum_copy, new_gain_copy):
        copy.wait_send()

    def drain_r(k, carry):
        r_copy((z + k) % RING).wait_send()
        return carry

    lax.fori_loop(1, RING, drain_r, 0)
    for copy in out_x + out_w:
        copy.wait()


def run(offset, call_id, inputs, cotangent, weight, gain):
    rows, width = inputs.shape
    feat, proj = weight.shape
    sizes = chunk_sizes(proj)
    any_space = pl.BlockSpec(memory_space=pl.ANY)
    vmem = pl.BlockSpec(memory_space=pltpu.VMEM)
    dma = pltpu.SemaphoreType.DMA

    def chunks(shape, dtype):
        return [pltpu.VMEM((*shape, n), dtype) for n in sizes]

    side = (COLS, width // COLS, rows)
    return pl.pallas_call(
        partial(body, offset),
        out_shape=(
            jax.ShapeDtypeStruct((rows, width), BF16),
            jax.ShapeDtypeStruct((feat, proj), BF16),
            jax.ShapeDtypeStruct((1, feat), F32),
        ),
        in_specs=[any_space, any_space, any_space, vmem],
        out_specs=(any_space, any_space, vmem),
        scratch_shapes=[
            chunks((RING, rows), BF16),
            chunks((COLS, feat), BF16),
            chunks((COLS, feat), F32),
            chunks((feat,), BF16),
            chunks((feat,), BF16),
            chunks((feat,), BF16),
            chunks((feat,), BF16),
            pltpu.VMEM((rows, width), BF16),
            pltpu.VMEM(side, BF16),
            pltpu.VMEM((RING, COLS, feat, rows), BF16),
            pltpu.VMEM((RING, COLS, feat, rows), BF16),
            pltpu.VMEM((RING, COLS, feat, rows), F32),
            pltpu.VMEM((COLS, feat, rows), F32),
            pltpu.VMEM((COLS, feat, 128), F32),
            pltpu.VMEM((RING, COLS, feat, rows), BF16),
            pltpu.VMEM(side, BF16),
            pltpu.VMEM((COLS, 8, 512), F32),
            pltpu.VMEM((3, 8, 512), F32),
            pltpu.VMEM((2, 8, 512), F32),
            dma((2 * CHUNKS + 1 + CHUNKS * PARTS,)),
            dma((14 * CHUNKS,)),
            dma((2 * RING * CHUNKS,)),
            dma((CHUNKS,)),
            dma((CHUNKS,)),
            dma((RING,)),
            dma((RING,)),
            dma((CHUNKS * PARTS,)),
            dma((CHUNKS * PARTS,)),
            dma((RING,)),
            dma((RING,)),
            dma((CHUNKS * PARTS,)),
            dma((CHUNKS * PARTS,)),
            dma((3,)),
            dma((3,)),
        ],
        compiler_params=pltpu.CompilerParams(
            collective_id=call_id, has_side_effects=True, vmem_limit_bytes=58 * 1024 * 1024
        ),
    )(inputs, cotangent, weight, gain)


def per_device(inputs, cotangent, weight, gain, step):
    levels = lax.axis_size("rep").bit_length() - 1
    exponent = jnp.remainder(step[0], levels)
    branches = [partial(run, 1 << level, 1 + level) for level in range(levels)]
    input_gradient, weight_out, gain_out = lax.switch(
        exponent, branches, inputs, cotangent, weight[0], gain
    )
    return (input_gradient, weight_out[None], gain_out.astype(BF16))


def solution(mesh):
    in_specs = (
        P(("rep", "fsdp"), None),
        P(("rep", "fsdp"), None),
        P("rep", "fsdp", None),
        P("rep", "fsdp"),
        P(),
    )
    out_specs = (P(("rep", "fsdp"), None), P("rep", "fsdp", None), P("rep", "fsdp"))
    return jax.shard_map(
        per_device, mesh=mesh, in_specs=in_specs, out_specs=out_specs, check_vma=False
    )
```
